32 devices in a mesh: group: 4 (over y, x), strip: 8 (over z, core).
Axes of the slice: x: 2, y: 2, z: 4, core: 2. Of those that a mesh axis runs over, the one named last changes fastest.
Arguments:
- initial: float32 [4, 256, 1024], P('group', 'strip'), may hold values from -6 to 6
- conductivity: float32 [4, 256, 1024], P('group', 'strip'), may hold values from 0.5 to 1.5
- step_count: int32 [4], P('group'), may hold values from 16 to 32, as said below
- emit_steps: int32 [4, 16], P('group'), may hold values from 1 to 32
- assign: int32 [128], replicated, may hold values from 0 to 63
- sample_inputs: bfloat16 [128, 128], P(('group', 'strip')), may hold values from -6 to 6
- w_first: bfloat16 [128, 512], replicated, may hold values from -0.5 to 0.5
- w_second: bfloat16 [512, 512], replicated, may hold values from -0.25 to 0.25
- w_third: bfloat16 [512, 512], replicated, may hold values from -0.25 to 0.25
- w_out: bfloat16 [512, 256, 1024], P(None, 'strip', 'group'), may hold values from -0.25 to 0.25
Outputs:
- grad_first: float32 [128, 512], replicated
- grad_second: float32 [512, 512], replicated
- grad_third: float32 [512, 512], replicated
- grad_out: bfloat16 [512, 256, 1024], P(None, 'strip', 'group')
The draws below stay inside these ranges and needn't reach their ends.
Inputs may be any that keep to these rules, and one draw needn't show every extreme that they name: `step_count`: at least 16; some field runs all 32 steps.
All inputs are finite; a program needn't handle non-finite values.
Results may differ from the reference program's by a relative error of at most 0.0039.
The reference program's roundings to bfloat16 on the way count: a program that leaves them out, or rounds other values in their place, can miss the bound.
Values may be sent and summed in bfloat16 or wider, within the bound.
No kernel may reach another device: no remote copies, remote signals or barrier semaphores. Data moves between devices by JAX's collectives and lax.ppermute only.
A program may use at most 64 MiB of HBM per device.

```python
import math
import jax
import jax.numpy as jnp
from jax import lax

ROWS_DEV = 32
NY = 1024
STEPS = 32
SNAPS = 16
HIDDEN_SIZE = 512
FEATURES = 128
FIELDS = 4
NX = 256
BATCH = 128


def draw_step_count(key, part):
    key_counts = jax.random.fold_in(key, 11)
    key_full = jax.random.fold_in(key, 12)
    counts = jax.random.randint(key_counts, (FIELDS,), STEPS // 2, STEPS + 1)
    full_field = jax.random.randint(key_full, (), 0, FIELDS)
    return jnp.where(jnp.arange(FIELDS) == full_field, STEPS, counts).astype(jnp.int32)


def draw_emit_steps(key, part):
    key_steps = jax.random.fold_in(key, 21)
    key_place = jax.random.fold_in(key, 22)
    emitted = jax.random.randint(key_steps, (FIELDS, SNAPS), 1, STEPS + 1)
    last_place = jax.random.randint(key_place, (FIELDS, 1), 0, SNAPS)
    first_place = (last_place + 1) % SNAPS
    columns = jnp.arange(SNAPS)[None, :]
    emitted = jnp.where(columns == last_place, STEPS, emitted)
    emitted = jnp.where(columns == first_place, 1, emitted)
    return emitted.astype(jnp.int32)


def place_ends(array, rng, smallest, high):
    longest = array.shape.index(max(array.shape))
    spots = []
    for shift in (0, 1):
        where = [jax.random.randint(jax.random.fold_in(rng, axis), (), 0, length) for axis, length in enumerate(array.shape)]
        where[longest] = (where[longest] + shift) % array.shape[longest]
        spots.append(tuple(where))
    return array.at[spots[0]].set(smallest).at[spots[1]].set(high)


def block_levels(stream_key, extent, shards, low, high):
    factor_of = 1.0
    for position, blocks in shards:
        steps = jax.random.uniform(jax.random.fold_in(jax.random.fold_in(stream_key, 6), position), (blocks,), jnp.float32, low / len(shards), high / len(shards))
        factor_of = factor_of * jnp.repeat(jnp.exp(steps), extent[position] // blocks).reshape((-1,) + (1,) * (len(extent) - 1 - position))
    return factor_of


def normal_values(own_key, extent, deviation, bound, shards=(), kind=jnp.bfloat16):
    gain = block_levels(own_key, extent, shards, -0.22, 0.18) if shards else 1.0
    values = jax.random.normal(own_key, extent, jnp.float32) * deviation * gain
    return jnp.minimum(jnp.maximum(values, -bound), bound).astype(kind)


def setup_inputs(seed: int = 0) -> dict:
    key_of = jax.random.split(jax.random.key(seed), 11)
    return {
        "initial": normal_values(key_of[0], (FIELDS, NX, NY), 1.0, 6.0, ((0, 4), (1, 8)), jnp.float32),
        "conductivity": jnp.clip(jnp.exp(math.log(1.5) - 1.0986123 * jax.random.uniform(key_of[1], (FIELDS, NX, NY), jnp.float32) ** block_levels(key_of[1], (FIELDS, NX, NY), ((0, 4), (1, 8)), -0.2, 0.2)), 0.5, 1.5),
        "step_count": draw_step_count(jax.random.fold_in(key_of[10], 71), 0),
        "emit_steps": draw_emit_steps(jax.random.fold_in(key_of[10], 71), 0),
        "assign": place_ends(jax.random.randint(key_of[4], (BATCH,), 0, FIELDS * SNAPS), jax.random.fold_in(key_of[4], 1), 0, (FIELDS * SNAPS) - 1).astype(jnp.int32),
        "sample_inputs": normal_values(key_of[5], (BATCH, FEATURES), 1.0, 6.0, ((0, 32),)),
        "w_first": normal_values(key_of[6], (FEATURES, HIDDEN_SIZE), FEATURES ** -0.5, 0.5),
        "w_second": normal_values(key_of[7], (HIDDEN_SIZE, HIDDEN_SIZE), HIDDEN_SIZE ** -0.5, 0.25),
        "w_third": normal_values(key_of[8], (HIDDEN_SIZE, HIDDEN_SIZE), HIDDEN_SIZE ** -0.5, 0.25),
        "w_out": normal_values(key_of[9], (HIDDEN_SIZE, NX, NY), HIDDEN_SIZE ** -0.5, 0.25, ((1, 8), (2, 4))),
    }


step_rate = 0.125

def evolve(initial, conductivity, step_count, emit_steps):

    def one_step(step_index, carried):
        field_now, snapshots = carried
        padded = jnp.pad(field_now, ((0, 0), (1, 1), (1, 1)))
        beside_all = padded[:, 2:, 1:-1] + padded[:, :-2, 1:-1] + padded[:, 1:-1, 2:] + padded[:, 1:-1, :-2]
        candidate = field_now + step_rate * conductivity * (1.0 + 0.25 * jnp.tanh(field_now)) * (beside_all - 4.0 * field_now)
        field_now = jnp.where((step_index < step_count)[:, None, None], candidate, field_now)
        matched = emit_steps == step_index + 1
        snapshots = jnp.where(matched[:, :, None, None], field_now[:, None], snapshots)
        return (field_now, snapshots)
    start_snaps = jnp.zeros((FIELDS, SNAPS, NX, NY), jnp.float32)
    field_now, snapshots = lax.fori_loop(0, STEPS, one_step, (initial, start_snaps))
    return snapshots.astype(jnp.bfloat16)

def contract_rows(left, right):
    return lax.dot_general(left, right, (((0,), (0,)), ((), ())), preferred_element_type=jnp.float32)

def contract_cols(left, right):
    return lax.dot_general(left, right, (((1,), (1,)), ((), ())), preferred_element_type=jnp.float32)

def reference(initial, conductivity, step_count, emit_steps, assign, sample_inputs, w_first, w_second, w_third, w_out):
    snapshots = evolve(initial, conductivity, step_count, emit_steps)
    flat_snaps = snapshots.reshape(FIELDS * SNAPS, NX, NY)
    act_a = jnp.tanh(jnp.dot(sample_inputs, w_first, preferred_element_type=jnp.float32))
    hidden_a = act_a.astype(jnp.bfloat16)
    act_b = jnp.tanh(jnp.dot(hidden_a, w_second, preferred_element_type=jnp.float32))
    hidden_b = act_b.astype(jnp.bfloat16)
    act_c = jnp.tanh(jnp.dot(hidden_b, w_third, preferred_element_type=jnp.float32))
    hidden_c = act_c.astype(jnp.bfloat16)
    inverse_root = 1.0 / jnp.sqrt(jnp.float32(BATCH))

    def block_fn(block_index):
        first_row = (block_index * ROWS_DEV).astype(jnp.int32)
        weight_block = lax.dynamic_slice_in_dim(w_out, first_row, ROWS_DEV, 1).reshape(HIDDEN_SIZE, ROWS_DEV * NY)
        snap_block = lax.dynamic_slice_in_dim(flat_snaps, first_row, ROWS_DEV, 1)
        target_block = jnp.take(snap_block, assign, axis=0).reshape(BATCH, ROWS_DEV * NY)
        predicted = jnp.dot(hidden_c, weight_block, preferred_element_type=jnp.float32)
        residual = ((predicted - target_block.astype(jnp.float32)) * inverse_root).astype(jnp.bfloat16)
        grad_block = contract_rows(hidden_c, residual).astype(jnp.bfloat16)
        back_block = contract_cols(residual, weight_block)
        return (grad_block.reshape(HIDDEN_SIZE, ROWS_DEV, NY), back_block)
    grad_blocks, back_blocks = lax.map(block_fn, jnp.arange(NX // ROWS_DEV, dtype=jnp.int32))
    grad_out = jnp.transpose(grad_blocks, (1, 0, 2, 3)).reshape(HIDDEN_SIZE, NX, NY)
    back_c = lax.optimization_barrier(jnp.sum(back_blocks, axis=0))
    delta_c = (back_c * (1.0 - act_c * act_c)).astype(jnp.bfloat16)
    grad_third = contract_rows(hidden_b, delta_c)
    back_b = contract_cols(delta_c, w_third)
    delta_b = (back_b * (1.0 - act_b * act_b)).astype(jnp.bfloat16)
    grad_second = contract_rows(hidden_a, delta_b)
    back_a = contract_cols(delta_b, w_second)
    delta_a = (back_a * (1.0 - act_a * act_a)).astype(jnp.bfloat16)
    grad_first = contract_rows(sample_inputs, delta_a)
    return (grad_first, grad_second, grad_third, grad_out)
```

```python
import functools

import jax
import jax.numpy as jnp
from jax import lax
from jax.experimental import pallas as pl
from jax.experimental.pallas import tpu as pltpu
from jax.sharding import PartitionSpec as P

STEPS = 32
LANES = 128
step_rate = 0.125

BF16 = jnp.bfloat16
F32 = jnp.float32
ALL = ("group", "strip")
whole = pl.BlockSpec(memory_space=pltpu.VMEM)
scalars = pl.BlockSpec(memory_space=pltpu.SMEM)


def params(mebibytes):
    return pltpu.CompilerParams(vmem_limit_bytes=mebibytes << 20)


def dot(left, right):
    return jnp.dot(left, right, preferred_element_type=F32)


def contract_rows(left, right):
    return lax.dot_general(left, right, (((0,), (0,)), ((), ())), preferred_element_type=F32)


def contract_cols(left, right):
    return lax.dot_general(left, right, (((1,), (1,)), ((), ())), preferred_element_type=F32)


def lane_tile(c):
    return slice(c * LANES, (c + 1) * LANES)


def split_kernel(count_ref, emit_ref, field_ref, kappa_ref, out_ref):
    blocks, _, rows, width = out_ref.shape
    cols = width - LANES
    lane = lax.broadcasted_iota(jnp.int32, (rows, LANES), 1)
    row = lax.broadcasted_iota(jnp.int32, (rows, LANES), 0)
    meta = jnp.zeros((rows, LANES), F32)
    for s in range(emit_ref.shape[1]):
        last = jnp.minimum(emit_ref[0, s], count_ref[0]) - 1
        meta = jnp.where((row == s) & (lane == STEPS), last.astype(F32), meta)
    none = jnp.zeros((rows, LANES), F32)
    for g in range(blocks):
        for part, ref in ((0, field_ref), (1, kappa_ref)):
            out_ref[g, part, :, :cols] = ref[0, :, g * cols : (g + 1) * cols]
            right = ref[0, :, (g + 1) * cols : (g + 1) * cols + LANES] if g < blocks - 1 else none
            left = ref[0, :, g * cols - LANES : g * cols] if g else none
            middle = meta if part == 0 else none
            out_ref[g, part, :, cols:] = jnp.where(
                lane < STEPS, right, jnp.where(lane >= LANES - STEPS, left, middle)
            )


def split_columns(initial, conductivity, step_count, emit_steps, blocks):
    _, rows, total = initial.shape
    width = total // blocks + LANES
    return pl.pallas_call(
        split_kernel,
        in_specs=[scalars, scalars, whole, whole],
        out_specs=whole,
        out_shape=jax.ShapeDtypeStruct((blocks, 2, rows, width), F32),
        compiler_params=params(16),
    )(step_count, emit_steps, initial, conductivity)


def solve_kernel(own_ref, top_ref, bottom_ref, out_ref, state, rate, bend, history):
    fields, _, rows, width = own_ref.shape
    tiles = width // LANES
    lane = lax.broadcasted_iota(jnp.int32, (8, LANES), 1)
    halo_lane = lax.broadcasted_iota(jnp.int32, (rows, LANES), 1)
    unused = (halo_lane >= STEPS) & (halo_lane < LANES - STEPS)
    first, last = lane == 0, lane == LANES - 1
    entries = fields * STEPS
    state[...] = jnp.zeros_like(state)

    def one_field(f, _):
        for j in range(tiles):
            for place, ref in enumerate((top_ref, own_ref, bottom_ref)):
                low = 8 + place * rows
                value = ref[f, 0, :, lane_tile(j)]
                if j == tiles - 1:
                    value = jnp.where(unused, 0.0, value)
                state[0, j, low : low + rows, :] = value
                kappa = ref[f, 1, :, lane_tile(j)] * step_rate
                rate[j, low : low + rows, :] = kappa
                bend[j, low : low + rows, :] = kappa * 0.25
        for part in range(STEPS // 8):

            def step(t, _):
                now = lax.rem(t, 2)
                later = 1 - now
                for tile in range(part, 3 * rows // 8 - part):
                    a = 8 + 8 * tile
                    middle = [state[now, j, a : a + 8, :] for j in range(tiles)]
                    west = [pltpu.roll(m, 1, 1) for m in middle]
                    east = [pltpu.roll(m, LANES - 1, 1) for m in middle]
                    for j in range(tiles):
                        beside = (state[now, j, a - 1 : a + 7, :] + state[now, j, a + 1 : a + 9, :]) + (
                            jnp.where(first, west[j - 1], west[j])
                            + jnp.where(last, east[(j + 1) % tiles], east[j])
                        )
                        gain = rate[j, a : a + 8, :] + bend[j, a : a + 8, :] * jnp.tanh(middle[j])
                        value = middle[j] + gain * (beside - 4.0 * middle[j])
                        state[later, j, a : a + 8, :] = value
                        if j < tiles - 1 and rows // 8 <= tile < 2 * rows // 8:
                            start = (8 * tile - rows) * entries + f * STEPS + t
                            history[j, pl.ds(start, 8, stride=entries), :] = value
                return 0

            lax.fori_loop(8 * part, 8 * part + 8, step, 0)
        return 0

    lax.fori_loop(0, fields, one_field, 0)
    out_ref[...] = history[...].astype(BF16)


def solve(own, top, bottom):
    fields, _, rows, width = own.shape
    tiles = width // LANES
    depth = 3 * rows + 16
    shape = (tiles - 1, rows * fields * STEPS, LANES)
    return pl.pallas_call(
        solve_kernel,
        in_specs=[whole, whole, whole],
        out_specs=whole,
        out_shape=jax.ShapeDtypeStruct(shape, BF16),
        scratch_shapes=[
            pltpu.VMEM((2, tiles, depth, LANES), F32),
            pltpu.VMEM((tiles, depth, LANES), F32),
            pltpu.VMEM((tiles, depth, LANES), F32),
            pltpu.VMEM(shape, F32),
        ],
        compiler_params=params(48),
    )(own, top, bottom)


def by_row_kernel(weight_ref, out_ref, wide):
    units, rows, cols = weight_ref.shape
    for c in range(cols // LANES):
        wide[c] = weight_ref[:, :, lane_tile(c)].astype(F32).reshape(units * rows, LANES)
    for r in range(rows):
        for c in range(cols // LANES):
            out_ref[r, :, lane_tile(c)] = wide[c, pl.ds(r, units, stride=rows), :].astype(BF16)


def by_row(weight, chunk=128):
    units, rows, cols = weight.shape
    return pl.pallas_call(
        by_row_kernel,
        grid=(units // chunk,),
        in_specs=[pl.BlockSpec((chunk, rows, cols), lambda i: (i, 0, 0))],
        out_specs=pl.BlockSpec((rows, chunk, cols), lambda i: (0, i, 0)),
        out_shape=jax.ShapeDtypeStruct((rows, units, cols), BF16),
        scratch_shapes=[pltpu.VMEM((cols // LANES, chunk * rows, LANES), F32)],
        compiler_params=params(32),
        cost_estimate=pl.CostEstimate(
            flops=0, bytes_accessed=4 * units * rows * cols, transcendentals=0
        ),
    )(weight)


def forward_kernel(inputs_ref, first_ref, second_ref, third_ref, a_ref, b_ref, c_ref, hid_ref):
    act = jnp.tanh(dot(inputs_ref[...], first_ref[...]))
    a_ref[...] = act
    act = jnp.tanh(dot(act.astype(BF16), second_ref[...]))
    b_ref[...] = act
    act = jnp.tanh(dot(act.astype(BF16), third_ref[...]))
    c_ref[...] = act
    hid_ref[...] = act.astype(BF16)


def forward(inputs, w_first, w_second, w_third):
    shape = (inputs.shape[0], w_first.shape[1])
    return pl.pallas_call(
        forward_kernel,
        in_specs=[whole] * 4,
        out_specs=[whole] * 4,
        out_shape=[jax.ShapeDtypeStruct(shape, F32)] * 3 + [jax.ShapeDtypeStruct(shape, BF16)],
        compiler_params=params(32),
    )(inputs, w_first, w_second, w_third)


def residual_kernel(scale, snaps, assign_ref, own_ref, hid_ref, weight_ref, history_ref, res_ref, back_ref, hot):
    rows, _, cols = weight_ref.shape
    fields = own_ref.shape[0]
    entries = fields * STEPS
    batch = hid_ref.shape[0]

    @pl.when(pl.program_id(0) == 0)
    def _():
        back_ref[...] = jnp.zeros_like(back_ref)
        lane = lax.broadcasted_iota(jnp.int32, (snaps, entries), 1)
        parts = []
        for f in range(fields):
            last = own_ref[f, 0, :snaps, STEPS : STEPS + 1].astype(jnp.int32)
            parts.append((lane == f * STEPS + last).astype(F32))
        steps = jnp.concatenate(parts, axis=0).astype(BF16)
        number = lax.broadcasted_iota(jnp.int32, (fields * snaps, batch), 0)
        chosen = (number == assign_ref[...]).astype(F32).astype(BF16)
        hot[...] = contract_rows(chosen, steps).astype(BF16)

    total = None
    for r in range(rows):
        predicted = dot(hid_ref[...], weight_ref[r])
        place = slice(r * entries, (r + 1) * entries)
        targets = [dot(hot[...], history_ref[c, place, :]) for c in range(cols // LANES)]
        residual = ((predicted - jnp.concatenate(targets, axis=1)) * scale).astype(BF16)
        res_ref[r] = residual
        back = contract_cols(residual, weight_ref[r])
        total = back if total is None else total + back
    back_ref[...] += total


def residual(assign, own, hidden, weight, history, snaps, chunk=4):
    rows, units, cols = weight.shape
    batch = hidden.shape[0]
    fields, _, _, width = own.shape
    entries = fields * STEPS
    scale = 1.0 / float(batch) ** 0.5
    return pl.pallas_call(
        functools.partial(residual_kernel, scale, snaps),
        grid=(rows // chunk,),
        in_specs=[
            pl.BlockSpec((1, batch), lambda i: (0, 0)),
            pl.BlockSpec((fields, 1, rows, LANES), lambda i: (0, 0, 0, width // LANES - 1)),
            pl.BlockSpec((batch, units), lambda i: (0, 0)),
            pl.BlockSpec((chunk, units, cols), lambda i: (i, 0, 0)),
            pl.BlockSpec((cols // LANES, chunk * entries, LANES), lambda i: (0, i, 0)),
        ],
        out_specs=[
            pl.BlockSpec((chunk, batch, cols), lambda i: (i, 0, 0)),
            pl.BlockSpec((batch, units), lambda i: (0, 0)),
        ],
        out_shape=[
            jax.ShapeDtypeStruct((rows, batch, cols), BF16),
            jax.ShapeDtypeStruct((batch, units), F32),
        ],
        scratch_shapes=[pltpu.VMEM((batch, entries), BF16)],
        compiler_params=params(48),
    )(assign.reshape(1, batch), own, hidden, weight, history)


def outer_kernel(hid_ref, res_ref, out_ref, wide):
    rows, _, cols = res_ref.shape
    units = out_ref.shape[0]
    for r in range(rows):
        grad = contract_rows(hid_ref[...], res_ref[r])
        for c in range(cols // LANES):
            wide[c, pl.ds(r, units, stride=rows), :] = grad[:, lane_tile(c)]
    for c in range(cols // LANES):
        out_ref[:, :, lane_tile(c)] = wide[c].reshape(units, rows, LANES).astype(BF16)


def outer(hidden, res, chunk=128):
    rows, batch, cols = res.shape
    units = hidden.shape[1]
    return pl.pallas_call(
        outer_kernel,
        grid=(units // chunk,),
        in_specs=[
            pl.BlockSpec((batch, chunk), lambda i: (0, i)),
            pl.BlockSpec((rows, batch, cols), lambda i: (0, 0, 0)),
        ],
        out_specs=pl.BlockSpec((chunk, rows, cols), lambda i: (i, 0, 0)),
        out_shape=jax.ShapeDtypeStruct((units, rows, cols), BF16),
        scratch_shapes=[pltpu.VMEM((cols // LANES, chunk * rows, LANES), F32)],
        compiler_params=params(48),
        cost_estimate=pl.CostEstimate(
            flops=2 * batch * units * rows * cols,
            bytes_accessed=4 * units * rows * cols,
            transcendentals=0,
        ),
    )(hidden, res)


def backward_kernel(inputs_ref, a_ref, b_ref, delta_ref, second_ref, third_ref, g1_ref, g2_ref, g3_ref):
    delta = delta_ref[...]
    act = b_ref[...]
    g3_ref[...] = contract_rows(act.astype(BF16), delta)
    delta = (contract_cols(delta, third_ref[...]) * (1.0 - act * act)).astype(BF16)
    act = a_ref[...]
    g2_ref[...] = contract_rows(act.astype(BF16), delta)
    delta = (contract_cols(delta, second_ref[...]) * (1.0 - act * act)).astype(BF16)
    g1_ref[...] = contract_rows(inputs_ref[...], delta)


def backward(inputs, act_a, act_b, delta, w_second, w_third):
    units = act_a.shape[1]
    return pl.pallas_call(
        backward_kernel,
        in_specs=[whole] * 6,
        out_specs=[whole] * 3,
        out_shape=[
            jax.ShapeDtypeStruct((inputs.shape[1], units), F32),
            jax.ShapeDtypeStruct((units, units), F32),
            jax.ShapeDtypeStruct((units, units), F32),
        ],
        compiler_params=params(32),
    )(inputs, act_a, act_b, delta, w_second, w_third)


def spread(block, count):
    copies = jnp.broadcast_to(block[None], (count,) + block.shape)
    got = lax.all_to_all(copies, ALL, split_axis=0, concat_axis=0, tiled=True)
    return got.reshape((-1,) + block.shape[1:])


def per_device(
    initial,
    conductivity,
    step_count,
    emit_steps,
    assign,
    sample_inputs,
    w_first,
    w_second,
    w_third,
    w_out,
):
    groups, strips = lax.axis_size("group"), lax.axis_size("strip")
    devices = groups * strips
    here = sample_inputs.shape[0]
    blocks = split_columns(initial, conductivity, step_count, emit_steps, groups)
    own = lax.all_to_all(blocks, "group", split_axis=0, concat_axis=0, tiled=True)
    down = [(i, i + 1) for i in range(strips - 1)]
    top = lax.ppermute(own, "strip", down)
    bottom = lax.ppermute(own, "strip", [(j, i) for i, j in down])
    inputs = spread(sample_inputs, devices)
    weight = by_row(w_out)
    act_a, act_b, act_c, hidden = forward(inputs, w_first, w_second, w_third)
    history = solve(own, top, bottom)
    res, partial = residual(assign, own, hidden, weight, history, emit_steps.shape[1])
    pieces = lax.all_to_all(
        partial.reshape(devices, here, -1), ALL, split_axis=0, concat_axis=0, tiled=True
    )
    grad_out = outer(hidden, res)
    mine = lax.axis_index(ALL) * here
    act_mine = lax.dynamic_slice_in_dim(act_c, mine, here, 0)
    delta_mine = (jnp.sum(pieces, axis=0) * (1.0 - act_mine * act_mine)).astype(BF16)
    delta = spread(delta_mine, devices)
    grads = backward(inputs, act_a, act_b, delta, w_second, w_third)
    return (*grads, grad_out)


def solution(mesh):
    placed = (
        P("group", "strip", None),
        P("group", "strip", None),
        P("group"),
        P("group", None),
        P(),
        P(("group", "strip"), None),
        P(),
        P(),
        P(),
        P(None, "strip", "group"),
    )
    return jax.shard_map(
        per_device,
        mesh=mesh,
        in_specs=placed,
        out_specs=(P(), P(), P(), P(None, "strip", "group")),
        check_vma=False,
    )
```

```python
import functools

import jax
import jax.numpy as jnp
from jax import lax
from jax.experimental import pallas as pl
from jax.experimental.pallas import tpu as pltpu
from jax.sharding import PartitionSpec as P

STEPS = 32
LANES = 128
META = 120
step_rate = 0.125

BF16 = jnp.bfloat16
F32 = jnp.float32
ALL = ("group", "strip")
whole = pl.BlockSpec(memory_space=pltpu.VMEM)
scalars = pl.BlockSpec(memory_space=pltpu.SMEM)


def params(mebibytes):
    return pltpu.CompilerParams(vmem_limit_bytes=mebibytes << 20)


def dot(left, right):
    return jnp.dot(left, right, preferred_element_type=F32)


def contract_rows(left, right):
    return lax.dot_general(left, right, (((0,), (0,)), ((), ())), preferred_element_type=F32)


def contract_cols(left, right):
    return lax.dot_general(left, right, (((1,), (1,)), ((), ())), preferred_element_type=F32)


def lane_tile(c):
    return slice(c * LANES, (c + 1) * LANES)


def tiles_for(cols):
    return -(-(cols + 2 * STEPS) // LANES)


def split_kernel(count_ref, emit_ref, field_ref, kappa_ref, inputs_ref, out_ref, seed_ref):
    blocks, _, rows, width = out_ref.shape
    tiles = width // LANES
    total = field_ref.shape[2]
    cols = total // blocks
    span = cols + 2 * LANES
    source = lax.broadcasted_iota(jnp.int32, (span, width), 0) - (LANES - STEPS)
    place = lax.broadcasted_iota(jnp.int32, (span, width), 1)
    wanted = tiles * (place % LANES) + place // LANES
    deal = ((source == wanted) & (wanted < cols + 2 * STEPS)).astype(F32).astype(BF16)
    none = jnp.zeros((2 * rows, LANES), F32)
    both = jnp.concatenate([field_ref[0], kappa_ref[0]], axis=0)
    both = jnp.concatenate([none, both, none], axis=1)
    high = both.astype(BF16)
    rest = both - high.astype(F32)
    middle = rest.astype(BF16)
    low = (rest - middle.astype(F32)).astype(BF16)
    lane = lax.broadcasted_iota(jnp.int32, (rows, LANES), 1)
    row = lax.broadcasted_iota(jnp.int32, (rows, LANES), 0)
    meta = jnp.zeros((rows, LANES), F32)
    for s in range(emit_ref.shape[1]):
        last = jnp.minimum(emit_ref[0, s], count_ref[0]) - 1
        meta = jnp.where(row == s, last.astype(F32), meta)
    for g in range(blocks):
        window = slice(g * cols, g * cols + span)
        dealt = dot(high[:, window], deal) + dot(middle[:, window], deal) + dot(low[:, window], deal)
        out_ref[g, 0] = dealt[:rows]
        out_ref[g, 1] = dealt[rows:]
        out_ref[g, 0, :, :LANES] = jnp.where(lane == META, meta, dealt[:rows, :LANES])
    here = inputs_ref.shape[0]
    devices, deep, features = seed_ref.shape
    seed = inputs_ref[...].astype(F32)
    if deep > here:
        seed = jnp.concatenate([seed, jnp.zeros((deep - here, features), F32)], axis=0)
    for d in range(devices):
        seed_ref[d] = seed


def split_columns(initial, conductivity, step_count, emit_steps, inputs, blocks, devices):
    _, rows, total = initial.shape
    width = tiles_for(total // blocks) * LANES
    here, features = inputs.shape
    return pl.pallas_call(
        split_kernel,
        in_specs=[scalars, scalars, whole, whole, whole],
        out_specs=[whole, whole],
        out_shape=[
            jax.ShapeDtypeStruct((blocks, 2, rows, width), F32),
            jax.ShapeDtypeStruct((devices, -(-here // 8) * 8, features), F32),
        ],
        compiler_params=params(60),
    )(step_count, emit_steps, initial, conductivity, inputs)


def advance(state, rate, bend, history, pitch, part, fields, now, t):
    _, _, tiles, depth, _ = state.shape
    rows = (depth - 16) // 3
    later = 1 - now
    for tile in range(part, 3 * rows // 8 - part):
        a = 8 + 8 * tile
        for f in fields:
            middle = [state[f, now, j, a : a + 8, :] for j in range(tiles)]
            west = [pltpu.roll(middle[-1], 1, 1)] + middle[:-1]
            east = middle[1:] + [pltpu.roll(middle[0], LANES - 1, 1)]
            for j in range(tiles):
                north = state[f, now, j, a - 1 : a + 7, :]
                south = state[f, now, j, a + 1 : a + 9, :]
                beside = (north + south) + (west[j] + east[j])
                gain = rate[f, j, a : a + 8, :] + bend[f, j, a : a + 8, :] * jnp.tanh(middle[j])
                value = middle[j] + gain * (beside - 4.0 * middle[j])
                state[f, later, j, a : a + 8, :] = value
                if rows <= 8 * tile < 2 * rows:
                    start = (8 * tile - rows) * pitch + f * STEPS + t
                    history[j, pl.ds(start, 8, stride=pitch), :] = value


def residual_kernel(
    scale, snaps, assign_ref, own_ref, top_ref, bottom_ref, predicted_ref, weight_ref,
    res_ref, back_ref, state, rate, bend, history, picked, weight, total, arrived,
):
    fields, _, rows, width = own_ref.shape
    _, batch, cols = predicted_ref.shape
    tiles = width // LANES
    entries = fields * STEPS
    pitch = entries + 1
    copy = pltpu.make_async_copy(weight_ref, weight, arrived)
    copy.start()

    state[...] = jnp.zeros_like(state)
    for f in range(fields):
        for j in range(tiles):
            for place, ref in enumerate((top_ref, own_ref, bottom_ref)):
                low = 8 + place * rows
                state[f, 0, j, low : low + rows, :] = ref[f, 0, :, lane_tile(j)]
                kappa = ref[f, 1, :, lane_tile(j)] * step_rate
                rate[f, j, low : low + rows, :] = kappa
                bend[f, j, low : low + rows, :] = kappa * 0.25
    together = 2 if fields % 2 == 0 else 1

    def some_fields(g, _):
        which = [g * together + i for i in range(together)]
        for part in range(STEPS // 8):

            def two_steps(pair, _):
                for now in range(2):
                    advance(state, rate, bend, history, pitch, part, which, now, 2 * pair + now)
                return 0

            lax.fori_loop(4 * part, 4 * part + 4, two_steps, 0)
        return 0

    lax.fori_loop(0, fields // together, some_fields, 0)

    lane = lax.broadcasted_iota(jnp.int32, (snaps, entries), 1)
    steps = []
    for f in range(fields):
        last = own_ref[f, 0, :snaps, META : META + 1].astype(jnp.int32)
        steps.append((lane == f * STEPS + last).astype(F32))
    steps = jnp.concatenate(steps, axis=0).astype(BF16)
    number = lax.broadcasted_iota(jnp.int32, (fields * snaps, batch), 0)
    chosen = (number == assign_ref[...]).astype(F32).astype(BF16)
    hot = contract_rows(chosen, steps).astype(BF16)
    place = lax.broadcasted_iota(jnp.int32, (width, cols), 0)
    column = lax.broadcasted_iota(jnp.int32, (width, cols), 1) + STEPS
    gather = (tiles * (place % LANES) + place // LANES == column).astype(F32).astype(BF16)

    for r in range(rows):
        for j in range(tiles):
            states = history[j, r * pitch : r * pitch + entries, :].astype(BF16)
            picked[r, :, lane_tile(j)] = dot(hot, states).astype(BF16)
    copy.wait()
    total[...] = jnp.zeros_like(total)

    def some_rows(i, _):
        back = None
        for k in range(chunk):
            r = i * chunk + k
            targets = dot(picked[r], gather)
            residual = ((predicted_ref[r] - targets) * scale).astype(BF16)
            res_ref[r] = residual
            part = contract_cols(residual, weight[r])
            back = part if back is None else back + part
        total[...] += back
        return 0

    chunk = 8
    lax.fori_loop(0, rows // chunk, some_rows, 0)
    devices, _, folded = back_ref.shape
    here = batch // devices
    for d in range(devices):
        for k in range(total.shape[1] // folded):
            back_ref[d, k * here : (k + 1) * here, :] = total[
                d * here : (d + 1) * here, k * folded : (k + 1) * folded
            ]


def residual(assign, own, top, bottom, predicted, weight, snaps, devices, fold):
    rows, units, cols = weight.shape
    batch = predicted.shape[1]
    fields, _, _, width = own.shape
    tiles = width // LANES
    depth = 3 * rows + 16
    entries = fields * STEPS
    here = batch // devices
    scale = 1.0 / float(batch) ** 0.5
    return pl.pallas_call(
        functools.partial(residual_kernel, scale, snaps),
        in_specs=[whole] * 5 + [pl.BlockSpec(memory_space=pl.ANY)],
        out_specs=[whole, whole],
        out_shape=[
            jax.ShapeDtypeStruct((rows, batch, cols), BF16),
            jax.ShapeDtypeStruct((devices, here * fold, units // fold), F32),
        ],
        scratch_shapes=[
            pltpu.VMEM((fields, 2, tiles, depth, LANES), F32),
            pltpu.VMEM((fields, tiles, depth, LANES), F32),
            pltpu.VMEM((fields, tiles, depth, LANES), F32),
            pltpu.VMEM((tiles, rows * (entries + 1), LANES), F32),
            pltpu.VMEM((rows, batch, width), BF16),
            pltpu.VMEM((rows, units, cols), BF16),
            pltpu.VMEM((batch, units), F32),
            pltpu.SemaphoreType.DMA,
        ],
        compiler_params=params(60),
    )(assign.reshape(1, batch), own, top, bottom, predicted, weight)


def by_row_kernel(weight_ref, out_ref):
    units, rows, cols = weight_ref.shape
    for c in range(cols // LANES):
        for u in range(0, units, 16):
            for r in range(0, rows, 16):
                block = weight_ref[u : u + 16, r : r + 16, lane_tile(c)]
                out_ref[r : r + 16, u : u + 16, lane_tile(c)] = jnp.swapaxes(block, 0, 1)


def by_row(weight, chunk=128):
    units, rows, cols = weight.shape
    return pl.pallas_call(
        by_row_kernel,
        grid=(units // chunk,),
        in_specs=[pl.BlockSpec((chunk, rows, cols), lambda i: (i, 0, 0))],
        out_specs=pl.BlockSpec((rows, chunk, cols), lambda i: (0, i, 0)),
        out_shape=jax.ShapeDtypeStruct((rows, units, cols), BF16),
        compiler_params=params(60),
        cost_estimate=pl.CostEstimate(
            flops=0, bytes_accessed=4 * units * rows * cols, transcendentals=0
        ),
    )(weight)


def fold_rows(value, out_ref, scratch):
    devices, deep, folded = out_ref.shape
    batch, units = value.shape
    here = batch // devices
    scratch[...] = value
    for d in range(devices):
        for k in range(units // folded):
            out_ref[d, k * here : (k + 1) * here, :] = scratch[
                d * here : (d + 1) * here, k * folded : (k + 1) * folded
            ]


def forward_kernel(
    seed_ref, first_ref, second_ref, third_ref, in_ref, a_ref, b_ref, hid_ref, gate_ref, inputs, scratch
):
    devices = seed_ref.shape[0]
    here = in_ref.shape[0] // devices
    for d in range(devices):
        inputs[d * here : (d + 1) * here, :] = seed_ref[d, :here, :]
    in_ref[...] = inputs[...].astype(BF16)
    act = jnp.tanh(dot(in_ref[...], first_ref[...]))
    a_ref[...] = act
    act = jnp.tanh(dot(act.astype(BF16), second_ref[...]))
    b_ref[...] = act
    act = jnp.tanh(dot(act.astype(BF16), third_ref[...]))
    hid_ref[...] = act.astype(BF16)
    fold_rows(1.0 - act * act, gate_ref, scratch)


def forward(seeds, w_first, w_second, w_third, here, fold):
    devices = seeds.shape[0]
    features, units = w_first.shape
    batch = devices * here
    shape = (batch, units)
    return pl.pallas_call(
        forward_kernel,
        in_specs=[whole] * 4,
        out_specs=[whole] * 5,
        out_shape=[
            jax.ShapeDtypeStruct((batch, features), BF16),
            jax.ShapeDtypeStruct(shape, F32),
            jax.ShapeDtypeStruct(shape, F32),
            jax.ShapeDtypeStruct(shape, BF16),
            jax.ShapeDtypeStruct((devices, here * fold, units // fold), F32),
        ],
        scratch_shapes=[pltpu.VMEM((batch, features), F32), pltpu.VMEM(shape, F32)],
        compiler_params=params(60),
    )(seeds, w_first, w_second, w_third)


def predict_kernel(hid_ref, weight_ref, out_ref):
    for r in range(weight_ref.shape[0]):
        out_ref[r] = dot(hid_ref[...], weight_ref[r])


def predict(hidden, weight, chunk=8):
    rows, units, cols = weight.shape
    batch = hidden.shape[0]
    return pl.pallas_call(
        predict_kernel,
        grid=(rows // chunk,),
        in_specs=[
            pl.BlockSpec((batch, units), lambda i: (0, 0)),
            pl.BlockSpec((chunk, units, cols), lambda i: (i, 0, 0)),
        ],
        out_specs=pl.BlockSpec((chunk, batch, cols), lambda i: (i, 0, 0)),
        out_shape=jax.ShapeDtypeStruct((rows, batch, cols), F32),
        compiler_params=params(60),
    )(hidden, weight)


def outer_kernel(hid_ref, res_ref, out_ref, grads):
    rows, _, cols = res_ref.shape
    units = out_ref.shape[0]
    for r in range(rows):
        grads[r] = contract_rows(hid_ref[...], res_ref[r]).astype(BF16)
    for c in range(cols // LANES):
        for u in range(0, units, 16):
            for r in range(0, rows, 16):
                block = grads[r : r + 16, u : u + 16, lane_tile(c)]
                out_ref[u : u + 16, r : r + 16, lane_tile(c)] = jnp.swapaxes(block, 0, 1)


def outer(hidden, res, chunk=128):
    rows, batch, cols = res.shape
    units = hidden.shape[1]
    return pl.pallas_call(
        outer_kernel,
        grid=(units // chunk,),
        in_specs=[
            pl.BlockSpec((batch, chunk), lambda i: (0, i)),
            pl.BlockSpec((rows, batch, cols), lambda i: (0, 0, 0)),
        ],
        out_specs=pl.BlockSpec((chunk, rows, cols), lambda i: (i, 0, 0)),
        out_shape=jax.ShapeDtypeStruct((units, rows, cols), BF16),
        scratch_shapes=[pltpu.VMEM((rows, chunk, cols), BF16)],
        compiler_params=params(60),
        cost_estimate=pl.CostEstimate(
            flops=2 * batch * units * rows * cols,
            bytes_accessed=4 * units * rows * cols,
            transcendentals=0,
        ),
    )(hidden, res)


def delta_kernel(here_ref, pieces_ref, gate_ref, out_ref):
    devices = pieces_ref.shape[0]
    back = pieces_ref[0]
    for d in range(1, devices):
        back = back + pieces_ref[d]
    delta = (back * gate_ref[here_ref[0]]).astype(BF16)
    for d in range(devices):
        out_ref[d] = delta


def delta_spread(place, pieces, gate):
    return pl.pallas_call(
        delta_kernel,
        in_specs=[scalars, whole, whole],
        out_specs=whole,
        out_shape=jax.ShapeDtypeStruct(pieces.shape, BF16),
        compiler_params=params(60),
    )(place.reshape(1), pieces, gate)


def backward_kernel(
    inputs_ref, a_ref, b_ref, delta_ref, second_ref, third_ref, g1_ref, g2_ref, g3_ref, folded, unfolded
):
    devices, deep, width = delta_ref.shape
    batch, units = a_ref.shape
    here = batch // devices
    folded[...] = delta_ref[...].astype(F32)
    for d in range(devices):
        for k in range(units // width):
            unfolded[d * here : (d + 1) * here, k * width : (k + 1) * width] = folded[
                d, k * here : (k + 1) * here, :
            ]
    delta = unfolded[...].astype(BF16)
    act = b_ref[...]
    g3_ref[...] = contract_rows(act.astype(BF16), delta)
    delta = (contract_cols(delta, third_ref[...]) * (1.0 - act * act)).astype(BF16)
    act = a_ref[...]
    g2_ref[...] = contract_rows(act.astype(BF16), delta)
    delta = (contract_cols(delta, second_ref[...]) * (1.0 - act * act)).astype(BF16)
    g1_ref[...] = contract_rows(inputs_ref[...], delta)


def backward(inputs, act_a, act_b, delta, w_second, w_third):
    batch, units = act_a.shape
    return pl.pallas_call(
        backward_kernel,
        in_specs=[whole] * 6,
        out_specs=[whole] * 3,
        out_shape=[
            jax.ShapeDtypeStruct((inputs.shape[1], units), F32),
            jax.ShapeDtypeStruct((units, units), F32),
            jax.ShapeDtypeStruct((units, units), F32),
        ],
        scratch_shapes=[pltpu.VMEM(delta.shape, F32), pltpu.VMEM((batch, units), F32)],
        compiler_params=params(60),
    )(inputs, act_a, act_b, delta, w_second, w_third)


def swap(value, axes):
    return lax.all_to_all(value, axes, split_axis=0, concat_axis=0, tiled=True)


def per_device(
    initial,
    conductivity,
    step_count,
    emit_steps,
    assign,
    sample_inputs,
    w_first,
    w_second,
    w_third,
    w_out,
):
    groups, strips = lax.axis_size("group"), lax.axis_size("strip")
    devices = groups * strips
    here = sample_inputs.shape[0]
    fold = max(1, 8 // here)
    blocks, seeds = split_columns(
        initial, conductivity, step_count, emit_steps, sample_inputs, groups, devices
    )
    blocks, seeds, w_out = lax.optimization_barrier((blocks, seeds, w_out))
    own = swap(blocks, "group")
    seeds = swap(seeds, ALL)
    weight = by_row(w_out)
    own, weight = lax.optimization_barrier((own, weight))
    down = [(i, i + 1) for i in range(strips - 1)]
    top = lax.ppermute(own, "strip", down)
    bottom = lax.ppermute(own, "strip", [(j, i) for i, j in down])
    inputs, act_a, act_b, hidden, gate = forward(seeds, w_first, w_second, w_third, here, fold)
    predicted = predict(hidden, weight)
    res, partial = residual(
        assign, own, top, bottom, predicted, weight, emit_steps.shape[1], devices, fold
    )
    pieces = swap(partial, ALL)
    grad_out = outer(hidden, res)
    pieces, grad_out = lax.optimization_barrier((pieces, grad_out))
    delta = swap(delta_spread(lax.axis_index(ALL), pieces, gate), ALL)
    grads = backward(inputs, act_a, act_b, delta, w_second, w_third)
    return (*grads, grad_out)


def solution(mesh):
    placed = (
        P("group", "strip", None),
        P("group", "strip", None),
        P("group"),
        P("group", None),
        P(),
        P(("group", "strip"), None),
        P(),
        P(),
        P(),
        P(None, "strip", "group"),
    )
    return jax.shard_map(
        per_device,
        mesh=mesh,
        in_specs=placed,
        out_specs=(P(), P(), P(), P(None, "strip", "group")),
        check_vma=False,
    )
```

```python
import functools

import jax
import jax.numpy as jnp
from jax import lax
from jax.experimental import pallas as pl
from jax.experimental.pallas import tpu as pltpu
from jax.sharding import PartitionSpec as P

STEPS = 32
LANES = 128
META = 120
step_rate = 0.125

BF16 = jnp.bfloat16
F32 = jnp.float32
ALL = ("group", "strip")
whole = pl.BlockSpec(memory_space=pltpu.VMEM)
scalars = pl.BlockSpec(memory_space=pltpu.SMEM)
far = pl.BlockSpec(memory_space=pl.ANY)


def params(mebibytes):
    return pltpu.CompilerParams(vmem_limit_bytes=mebibytes << 20)


def dot(left, right):
    return jnp.dot(left, right, preferred_element_type=F32)


def contract_rows(left, right):
    return lax.dot_general(left, right, (((0,), (0,)), ((), ())), preferred_element_type=F32)


def contract_cols(left, right):
    return lax.dot_general(left, right, (((1,), (1,)), ((), ())), preferred_element_type=F32)


def lane_tile(c):
    return slice(c * LANES, (c + 1) * LANES)


def tiles_for(cols):
    return -(-(cols + 2 * STEPS) // LANES)


def split_kernel(
    count_ref, emit_ref, field_far, kappa_far, inputs_far, out_ref, seed_ref, field_ref, kappa_ref, inputs_ref, arrived
):
    loads = [
        pltpu.make_async_copy(source, target, arrived.at[i])
        for i, (source, target) in enumerate(
            ((field_far, field_ref), (kappa_far, kappa_ref), (inputs_far, inputs_ref))
        )
    ]
    for load in loads:
        load.start()
    blocks, _, rows, width = out_ref.shape
    tiles = width // LANES
    total = field_ref.shape[2]
    cols = total // blocks
    span = cols + 2 * LANES
    source = lax.broadcasted_iota(jnp.int32, (span, width), 0) - (LANES - STEPS)
    place = lax.broadcasted_iota(jnp.int32, (span, width), 1)
    wanted = tiles * (place % LANES) + place // LANES
    deal = ((source == wanted) & (wanted < cols + 2 * STEPS)).astype(F32).astype(BF16)
    for load in loads:
        load.wait()
    none = jnp.zeros((2 * rows, LANES), F32)
    both = jnp.concatenate([field_ref[0], kappa_ref[0] * step_rate], axis=0)
    both = jnp.concatenate([none, both, none], axis=1)
    high = both.astype(BF16)
    rest = both - high.astype(F32)
    middle = rest.astype(BF16)
    low = (rest - middle.astype(F32)).astype(BF16)
    lane = lax.broadcasted_iota(jnp.int32, (rows, LANES), 1)
    row = lax.broadcasted_iota(jnp.int32, (rows, LANES), 0)
    meta = jnp.zeros((rows, LANES), F32)
    for s in range(emit_ref.shape[1]):
        last = jnp.minimum(emit_ref[0, s], count_ref[0]) - 1
        meta = jnp.where(row == s, last.astype(F32), meta)
    windows = [slice(g * cols, g * cols + span) for g in range(blocks)]
    stacked = [part[:, window] for window in windows for part in (high, middle, low)]
    product = dot(jnp.concatenate(stacked, axis=0), deal)
    for g in range(blocks):
        parts = [product[2 * rows * (3 * g + i) : 2 * rows * (3 * g + i + 1)] for i in range(3)]
        dealt = parts[0] + parts[1] + parts[2]
        out_ref[g, 0] = dealt[:rows]
        out_ref[g, 1] = dealt[rows:]
        out_ref[g, 0, :, :LANES] = jnp.where(lane == META, meta, dealt[:rows, :LANES])
    here = inputs_ref.shape[0]
    devices, deep, features = seed_ref.shape
    seed = inputs_ref[...].astype(F32)
    if deep > here:
        seed = jnp.concatenate([seed, jnp.zeros((deep - here, features), F32)], axis=0)
    for d in range(devices):
        seed_ref[d] = seed


def split_columns(initial, conductivity, step_count, emit_steps, inputs, blocks, devices):
    _, rows, total = initial.shape
    width = tiles_for(total // blocks) * LANES
    here, features = inputs.shape
    return pl.pallas_call(
        split_kernel,
        in_specs=[scalars, scalars, far, far, far],
        out_specs=[whole, whole],
        out_shape=[
            jax.ShapeDtypeStruct((blocks, 2, rows, width), F32),
            jax.ShapeDtypeStruct((devices, -(-here // 8) * 8, features), F32),
        ],
        scratch_shapes=[
            pltpu.VMEM(initial.shape, F32),
            pltpu.VMEM(conductivity.shape, F32),
            pltpu.VMEM(inputs.shape, BF16),
            pltpu.SemaphoreType.DMA((3,)),
        ],
        compiler_params=params(63),
    )(step_count, emit_steps, initial, conductivity, inputs)


def advance(state, rate, history, pitch, part, fields, now, t):
    _, _, tiles, depth, _ = state.shape
    rows = (depth - 16) // 3
    later = 1 - now
    for tile in range(part, 3 * rows // 8 - part):
        a = 8 + 8 * tile
        for f in fields:
            middle = [state[f, now, j, a : a + 8, :] for j in range(tiles)]
            west = [pltpu.roll(middle[-1], 1, 1)] + middle[:-1]
            east = middle[1:] + [pltpu.roll(middle[0], LANES - 1, 1)]
            for j in range(tiles):
                north = state[f, now, j, a - 1 : a + 7, :]
                south = state[f, now, j, a + 1 : a + 9, :]
                beside = (north + south) + (west[j] + east[j])
                gain = rate[f, j, a : a + 8, :] * (1.0 + 0.25 * jnp.tanh(middle[j]))
                value = middle[j] + gain * (beside - 4.0 * middle[j])
                state[f, later, j, a : a + 8, :] = value
                if rows <= 8 * tile < 2 * rows:
                    start = (8 * tile - rows) * pitch + f * STEPS + t
                    history[j, pl.ds(start, 8, stride=pitch), :] = value


def fold_rows(value, out_ref):
    devices, deep, folded = out_ref.shape
    batch, units = value.shape
    here = batch // devices
    for d in range(devices):
        for k in range(units // folded):
            out_ref[d, k * here : (k + 1) * here, :] = value[
                d * here : (d + 1) * here, k * folded : (k + 1) * folded
            ]


def by_row_kernel(first, weight_far, out_far, weight, by_rows, arrived, left):
    pieces, units, rows, cols = weight.shape
    places = [slice(i * units, (i + 1) * units) for i in range(pieces)]
    sources = [slice(first + i * units, first + (i + 1) * units) for i in range(pieces)]
    loads = [
        pltpu.make_async_copy(weight_far.at[sources[i]], weight.at[i], arrived.at[i])
        for i in range(pieces)
    ]
    stores = [
        pltpu.make_async_copy(by_rows.at[i], out_far.at[:, places[i], :], left.at[i])
        for i in range(pieces)
    ]
    for load in loads:
        load.start()
    for i in range(pieces):
        loads[i].wait()

        def some_units(u, _):
            place = pl.ds(pl.multiple_of(u * 16, 16), 16)
            for c in range(cols // LANES):
                for r in range(0, rows, 16):
                    block = weight[i, place, r : r + 16, lane_tile(c)]
                    by_rows[i, r : r + 16, place, lane_tile(c)] = jnp.swapaxes(block, 0, 1)
            return 0

        lax.fori_loop(0, units // 16, some_units, 0)
        stores[i].start()
    for store in stores:
        store.wait()


def by_row(weight, half, pieces=4):
    units, rows, cols = weight.shape
    units = units // 2
    return pl.pallas_call(
        functools.partial(by_row_kernel, half * units),
        in_specs=[far],
        out_specs=far,
        out_shape=jax.ShapeDtypeStruct((rows, units, cols), BF16),
        scratch_shapes=[
            pltpu.VMEM((pieces, units // pieces, rows, cols), BF16),
            pltpu.VMEM((pieces, rows, units // pieces, cols), BF16),
            pltpu.SemaphoreType.DMA((pieces,)),
            pltpu.SemaphoreType.DMA((pieces,)),
        ],
        compiler_params=params(63),
        cost_estimate=pl.CostEstimate(
            flops=0, bytes_accessed=4 * units * rows * cols, transcendentals=0
        ),
    )(weight)


def forward(seed_ref, first_ref, second_ref, third_ref, inputs, act_a, act_b, hidden, gate, raw, scratch):
    devices = seed_ref.shape[0]
    here = inputs.shape[0] // devices
    for d in range(devices):
        raw[d * here : (d + 1) * here, :] = seed_ref[d, :here, :]
    inputs[...] = raw[...].astype(BF16)
    act = jnp.tanh(dot(inputs[...], first_ref[...]))
    act_a[...] = act
    act = jnp.tanh(dot(act.astype(BF16), second_ref[...]))
    act_b[...] = act
    act = jnp.tanh(dot(act.astype(BF16), third_ref[...]))
    hidden[...] = act.astype(BF16)
    scratch[...] = 1.0 - act * act
    fold_rows(scratch, gate)


def main_kernel(
    scale, snaps, own_far, top_far, bottom_far, seed_far, low_far, high_far, assign_far, first_far, second_far, third_far,
    res_far, back_ref, in_far, a_far, b_far, hid_far, gate_far,
    state, rate, history, picked, predicted, by_rows, total, raw, assigned, first, second, third,
    own_ref, top_ref, bottom_ref, seed_ref, res, inputs, act_a, act_b, hidden, gate, arrived, filled, left,
):
    fields, _, rows, width = own_ref.shape
    _, batch, cols = predicted.shape
    units = by_rows.shape[1]
    tiles = width // LANES
    entries = fields * STEPS
    pitch = entries + 1
    pairs = (
        (seed_far, seed_ref), (first_far, first), (second_far, second), (third_far, third),
        (top_far, top_ref), (own_far, own_ref), (bottom_far, bottom_ref), (assign_far, assigned),
    )
    loads = [
        pltpu.make_async_copy(source, target, arrived.at[i])
        for i, (source, target) in enumerate(pairs)
    ]
    for load in loads:
        load.start()
    together = 2 if fields % 2 == 0 else 1
    parts = STEPS // 8
    turns = fields // together * parts
    each = -(-rows // (4 * turns))
    fills = [
        [
            pltpu.make_async_copy(
                source.at[low : low + 4 * each],
                by_rows.at[low : low + 4 * each, half * units // 2 : (half + 1) * units // 2, :],
                filled.at[half, low // (4 * each)],
            )
            for half, source in enumerate((low_far, high_far))
        ]
        for low in range(0, rows, 4 * each)
    ]
    for pair in fills:
        for fill in pair:
            fill.start()
    for load in loads[:4]:
        load.wait()
    forward(seed_ref, first, second, third, inputs, act_a, act_b, hidden, gate, raw, total)
    stores = [
        pltpu.make_async_copy(source, target, left.at[i])
        for i, (source, target) in enumerate(
            ((inputs, in_far), (act_a, a_far), (act_b, b_far), (hidden, hid_far), (gate, gate_far))
        )
    ]
    for store in stores:
        store.start()
    for load in loads[4:]:
        load.wait()

    for f in range(fields):
        for now in range(2):
            for j in range(tiles):
                state[f, now, j, :8, :] = jnp.zeros((8, LANES), F32)
                state[f, now, j, 8 + 3 * rows :, :] = jnp.zeros((8, LANES), F32)
        for j in range(tiles):
            for place, ref in enumerate((top_ref, own_ref, bottom_ref)):
                low = 8 + place * rows
                state[f, 0, j, low : low + rows, :] = ref[f, 0, :, lane_tile(j)]
                rate[f, j, low : low + rows, :] = ref[f, 1, :, lane_tile(j)]
                if place != 1:
                    state[f, 1, j, low : low + rows, :] = ref[f, 0, :, lane_tile(j)]
    for turn in range(turns):
        if turn < len(fills):
            for fill in fills[turn]:
                fill.wait()
        which = [turn // parts * together + i for i in range(together)]
        part = turn % parts

        def two_steps(pair, _):
            for now in range(2):
                advance(state, rate, history, pitch, part, which, now, 2 * pair + now)
            if turn * 4 * each < rows:
                for k in range(each):
                    r = (turn * 4 + pair - 4 * part) * each + k
                    predicted[r] = dot(hidden[...], by_rows[r])
            return 0

        lax.fori_loop(4 * part, 4 * part + 4, two_steps, 0)

    lane = lax.broadcasted_iota(jnp.int32, (snaps, entries), 1)
    steps = []
    for f in range(fields):
        last = own_ref[f, 0, :snaps, META : META + 1].astype(jnp.int32)
        steps.append((lane == f * STEPS + last).astype(F32))
    steps = jnp.concatenate(steps, axis=0).astype(BF16)
    number = lax.broadcasted_iota(jnp.int32, (fields * snaps, batch), 0)
    chosen = (number == assigned[...]).astype(F32).astype(BF16)
    hot = contract_rows(chosen, steps).astype(BF16)
    place = lax.broadcasted_iota(jnp.int32, (width, cols), 0)
    column = lax.broadcasted_iota(jnp.int32, (width, cols), 1) + STEPS
    gather = (tiles * (place % LANES) + place // LANES == column).astype(F32).astype(BF16)

    chunk = 8
    for i in range(rows // chunk):
        for k in range(chunk):
            low = (i * chunk + k) * pitch
            for j in range(tiles):
                states = history[j, low : low + entries, :].astype(BF16)
                picked[k * batch : (k + 1) * batch, lane_tile(j)] = dot(hot, states).astype(BF16)
        targets = dot(picked[...], gather)
        back = None
        for k in range(chunk):
            r = i * chunk + k
            residual = ((predicted[r] - targets[k * batch : (k + 1) * batch]) * scale).astype(BF16)
            res[r] = residual
            part = contract_cols(residual, by_rows[r])
            back = part if back is None else back + part
        total[...] = back if i == 0 else total[...] + back
        place = slice(i * chunk, (i + 1) * chunk)
        stores.append(pltpu.make_async_copy(res.at[place], res_far.at[place], left.at[5 + i]))
        stores[-1].start()
    fold_rows(total, back_ref)
    for store in stores:
        store.wait()


def main(assign, own, top, bottom, seeds, w_first, w_second, w_third, halves, snaps, here, fold):
    rows, units, cols = halves[0].shape
    units = 2 * units
    features = w_first.shape[0]
    devices = seeds.shape[0]
    batch = devices * here
    fields, _, _, width = own.shape
    tiles = width // LANES
    depth = 3 * rows + 16
    entries = fields * STEPS
    scale = 1.0 / float(batch) ** 0.5
    folded = (devices, here * fold, units // fold)
    kept = [
        ((rows, batch, cols), BF16),
        ((batch, features), BF16),
        ((batch, units), F32),
        ((batch, units), F32),
        ((batch, units), BF16),
        (folded, F32),
    ]
    shapes = [jax.ShapeDtypeStruct(*k) for k in kept]
    return pl.pallas_call(
        functools.partial(main_kernel, scale, snaps),
        in_specs=[far] * 10,
        out_specs=[far, whole] + [far] * 5,
        out_shape=[shapes[0], jax.ShapeDtypeStruct(folded, F32)] + shapes[1:],
        scratch_shapes=[
            pltpu.VMEM((fields, 2, tiles, depth, LANES), F32),
            pltpu.VMEM((fields, tiles, depth, LANES), F32),
            pltpu.VMEM((tiles, rows * (entries + 1), LANES), F32),
            pltpu.VMEM((8 * batch, width), BF16),
            pltpu.VMEM((rows, batch, cols), F32),
            pltpu.VMEM((rows, units, cols), BF16),
            pltpu.VMEM((batch, units), F32),
            pltpu.VMEM((batch, features), F32),
            pltpu.VMEM((1, batch), jnp.int32),
            pltpu.VMEM(w_first.shape, BF16),
            pltpu.VMEM(w_second.shape, BF16),
            pltpu.VMEM(w_third.shape, BF16),
            pltpu.VMEM(own.shape, F32),
            pltpu.VMEM(own.shape, F32),
            pltpu.VMEM(own.shape, F32),
            pltpu.VMEM(seeds.shape, F32),
        ]
        + [pltpu.VMEM(*k) for k in kept]
        + [
            pltpu.SemaphoreType.DMA((8,)),
            pltpu.SemaphoreType.DMA((2, rows // 4)),
            pltpu.SemaphoreType.DMA((5 + rows // 8,)),
        ],
        compiler_params=params(63),
    )(own, top, bottom, seeds, *halves, assign.reshape(1, batch), w_first, w_second, w_third)


def outer_kernel(hid_ref, res_ref, out_ref, grads):
    rows, _, cols = res_ref.shape
    units = out_ref.shape[0]
    for r in range(rows):
        grads[r] = contract_rows(hid_ref[...], res_ref[r]).astype(BF16)
    for c in range(cols // LANES):
        for u in range(0, units, 16):
            for r in range(0, rows, 16):
                block = grads[r : r + 16, u : u + 16, lane_tile(c)]
                out_ref[u : u + 16, r : r + 16, lane_tile(c)] = jnp.swapaxes(block, 0, 1)


def outer(hidden, res, chunk=128):
    rows, batch, cols = res.shape
    units = hidden.shape[1]
    return pl.pallas_call(
        outer_kernel,
        grid=(units // chunk,),
        in_specs=[
            pl.BlockSpec((batch, chunk), lambda i: (0, i)),
            pl.BlockSpec((rows, batch, cols), lambda i: (0, 0, 0)),
        ],
        out_specs=pl.BlockSpec((chunk, rows, cols), lambda i: (i, 0, 0)),
        out_shape=jax.ShapeDtypeStruct((units, rows, cols), BF16),
        scratch_shapes=[pltpu.VMEM((rows, chunk, cols), BF16)],
        compiler_params=params(63),
        cost_estimate=pl.CostEstimate(
            flops=2 * batch * units * rows * cols,
            bytes_accessed=4 * units * rows * cols,
            transcendentals=0,
        ),
    )(hidden, res)


def delta_kernel(pieces_far, gate_far, out_ref, pieces, gate, arrived):
    devices = pieces.shape[0]
    loads = [
        pltpu.make_async_copy(pieces_far, pieces, arrived.at[0]),
        pltpu.make_async_copy(gate_far.at[lax.axis_index(ALL)], gate, arrived.at[1]),
    ]
    for load in loads:
        load.start()
    for load in loads:
        load.wait()
    back = [pieces[d] for d in range(devices)]
    while len(back) > 1:
        back = [a + b for a, b in zip(back[::2], back[1::2])] + back[len(back) // 2 * 2 :]
    delta = (back[0] * gate[...]).astype(BF16)
    for d in range(devices):
        out_ref[d] = delta


def delta_spread(pieces, gate):
    return pl.pallas_call(
        delta_kernel,
        in_specs=[far, far],
        out_specs=whole,
        out_shape=jax.ShapeDtypeStruct(pieces.shape, BF16),
        scratch_shapes=[
            pltpu.VMEM(pieces.shape, F32),
            pltpu.VMEM(gate.shape[1:], F32),
            pltpu.SemaphoreType.DMA((2,)),
        ],
        compiler_params=params(63),
    )(pieces, gate)


def backward_kernel(
    inputs_far, a_far, b_far, delta_far, second_far, third_far, g1_far, g2_far, g3_far,
    inputs, act_a, act_b, folded, second, third, wide, unfolded, g1, g2, g3, arrived, left,
):
    pairs = (
        (delta_far, folded), (b_far, act_b), (third_far, third),
        (a_far, act_a), (second_far, second), (inputs_far, inputs),
    )
    loads = [
        pltpu.make_async_copy(source, target, arrived.at[i])
        for i, (source, target) in enumerate(pairs)
    ]
    for load in loads:
        load.start()
    stores = [
        pltpu.make_async_copy(source, target, left.at[i])
        for i, (source, target) in enumerate(((g3, g3_far), (g2, g2_far), (g1, g1_far)))
    ]
    devices, deep, width = folded.shape
    batch, units = act_a.shape
    here = batch // devices
    loads[0].wait()
    wide[...] = folded[...].astype(F32)
    for d in range(devices):
        for k in range(units // width):
            unfolded[d * here : (d + 1) * here, k * width : (k + 1) * width] = wide[
                d, k * here : (k + 1) * here, :
            ]
    delta = unfolded[...].astype(BF16)
    loads[1].wait()
    act = act_b[...]
    g3[...] = contract_rows(act.astype(BF16), delta)
    stores[0].start()
    loads[2].wait()
    delta = (contract_cols(delta, third[...]) * (1.0 - act * act)).astype(BF16)
    loads[3].wait()
    act = act_a[...]
    g2[...] = contract_rows(act.astype(BF16), delta)
    stores[1].start()
    loads[4].wait()
    delta = (contract_cols(delta, second[...]) * (1.0 - act * act)).astype(BF16)
    loads[5].wait()
    g1[...] = contract_rows(inputs[...], delta)
    stores[2].start()
    for store in stores:
        store.wait()


def backward(inputs, act_a, act_b, delta, w_second, w_third):
    batch, units = act_a.shape
    shapes = [(inputs.shape[1], units), (units, units), (units, units)]
    return pl.pallas_call(
        backward_kernel,
        in_specs=[far] * 6,
        out_specs=[far] * 3,
        out_shape=[jax.ShapeDtypeStruct(shape, F32) for shape in shapes],
        scratch_shapes=[
            pltpu.VMEM(inputs.shape, BF16),
            pltpu.VMEM(act_a.shape, F32),
            pltpu.VMEM(act_b.shape, F32),
            pltpu.VMEM(delta.shape, BF16),
            pltpu.VMEM(w_second.shape, BF16),
            pltpu.VMEM(w_third.shape, BF16),
            pltpu.VMEM(delta.shape, F32),
            pltpu.VMEM((batch, units), F32),
        ]
        + [pltpu.VMEM(shape, F32) for shape in shapes]
        + [pltpu.SemaphoreType.DMA((6,)), pltpu.SemaphoreType.DMA((3,))],
        compiler_params=params(63),
    )(inputs, act_a, act_b, delta, w_second, w_third)


def swap(value, axes):
    return lax.all_to_all(value, axes, split_axis=0, concat_axis=0, tiled=True)


def per_device(
    initial,
    conductivity,
    step_count,
    emit_steps,
    assign,
    sample_inputs,
    w_first,
    w_second,
    w_third,
    w_out,
):
    groups, strips = lax.axis_size("group"), lax.axis_size("strip")
    devices = groups * strips
    here = sample_inputs.shape[0]
    fold = max(1, 8 // here)
    blocks, seeds = split_columns(
        initial, conductivity, step_count, emit_steps, sample_inputs, groups, devices
    )
    blocks, w_out = lax.optimization_barrier((blocks, w_out))
    own = swap(blocks, "group")
    low = by_row(w_out, 0)
    own, low, w_out = lax.optimization_barrier((own, low, w_out))
    down = [(i, i + 1) for i in range(strips - 1)]
    top = lax.ppermute(own, "strip", down)
    bottom = lax.ppermute(own, "strip", [(j, i) for i, j in down])
    own, seeds = lax.optimization_barrier((own, seeds))
    seeds = swap(seeds, ALL)
    res, partial, inputs, act_a, act_b, hidden, gate = main(
        assign, own, top, bottom, seeds, w_first, w_second, w_third, (low, by_row(w_out, 1)),
        emit_steps.shape[1], here, fold,
    )
    pieces = swap(partial, ALL)
    grad_out = outer(hidden, res)
    pieces, grad_out = lax.optimization_barrier((pieces, grad_out))
    delta = swap(delta_spread(pieces, gate), ALL)
    grads = backward(inputs, act_a, act_b, delta, w_second, w_third)
    return (*grads, grad_out)


def solution(mesh):
    placed = (
        P("group", "strip", None),
        P("group", "strip", None),
        P("group"),
        P("group", None),
        P(),
        P(("group", "strip"), None),
        P(),
        P(),
        P(),
        P(None, "strip", "group"),
    )
    return jax.shard_map(
        per_device,
        mesh=mesh,
        in_specs=placed,
        out_specs=(P(), P(), P(), P(None, "strip", "group")),
        check_vma=False,
    )
```

```python
import functools

import jax
import jax.numpy as jnp
from jax import lax
from jax.experimental import pallas as pl
from jax.experimental.pallas import tpu as pltpu
from jax.sharding import PartitionSpec as P

STEPS = 32
LANES = 128
META = 120
step_rate = 0.125

BF16 = jnp.bfloat16
F32 = jnp.float32
ALL = ("group", "strip")
whole = pl.BlockSpec(memory_space=pltpu.VMEM)
scalars = pl.BlockSpec(memory_space=pltpu.SMEM)
far = pl.BlockSpec(memory_space=pl.ANY)


def params(kibibytes=65024):
    return pltpu.CompilerParams(vmem_limit_bytes=kibibytes << 10)


def dot(left, right):
    return jnp.dot(left, right, preferred_element_type=F32)


def contract_rows(left, right):
    return lax.dot_general(left, right, (((0,), (0,)), ((), ())), preferred_element_type=F32)


def contract_cols(left, right):
    return lax.dot_general(left, right, (((1,), (1,)), ((), ())), preferred_element_type=F32)


def lane_tile(c):
    return slice(c * LANES, (c + 1) * LANES)


def tiles_for(cols):
    return -(-(cols + 2 * STEPS) // LANES)


def split_kernel(
    count_ref, emit_ref, field_far, kappa_far, inputs_far, out_ref, seed_ref, field_ref, kappa_ref, inputs_ref, arrived
):
    loads = [
        pltpu.make_async_copy(source, target, arrived.at[i])
        for i, (source, target) in enumerate(
            ((field_far, field_ref), (kappa_far, kappa_ref), (inputs_far, inputs_ref))
        )
    ]
    for load in loads:
        load.start()
    blocks, _, rows, width = out_ref.shape
    tiles = width // LANES
    total = field_ref.shape[2]
    cols = total // blocks
    span = cols + 2 * LANES
    source = lax.broadcasted_iota(jnp.int32, (span, width), 0) - (LANES - STEPS)
    place = lax.broadcasted_iota(jnp.int32, (span, width), 1)
    wanted = tiles * (place % LANES) + place // LANES
    deal = ((source == wanted) & (wanted < cols + 2 * STEPS)).astype(F32).astype(BF16)
    for load in loads:
        load.wait()
    none = jnp.zeros((2 * rows, LANES), F32)
    both = jnp.concatenate([field_ref[0], kappa_ref[0] * step_rate], axis=0)
    both = jnp.concatenate([none, both, none], axis=1)
    high = both.astype(BF16)
    rest = both - high.astype(F32)
    middle = rest.astype(BF16)
    low = (rest - middle.astype(F32)).astype(BF16)
    lane = lax.broadcasted_iota(jnp.int32, (rows, LANES), 1)
    row = lax.broadcasted_iota(jnp.int32, (rows, LANES), 0)
    meta = jnp.zeros((rows, LANES), F32)
    for s in range(emit_ref.shape[1]):
        last = jnp.minimum(emit_ref[0, s], count_ref[0]) - 1
        meta = jnp.where(row == s, last.astype(F32), meta)
    windows = [slice(g * cols, g * cols + span) for g in range(blocks)]
    stacked = [part[:, window] for window in windows for part in (high, middle, low)]
    product = dot(jnp.concatenate(stacked, axis=0), deal)
    for g in range(blocks):
        parts = [product[2 * rows * (3 * g + i) : 2 * rows * (3 * g + i + 1)] for i in range(3)]
        dealt = parts[0] + parts[1] + parts[2]
        out_ref[g, 0] = dealt[:rows]
        out_ref[g, 1] = dealt[rows:]
        out_ref[g, 0, :, :LANES] = jnp.where(lane == META, meta, dealt[:rows, :LANES])
    here = inputs_ref.shape[0]
    devices, deep, features = seed_ref.shape
    seed = inputs_ref[...].astype(F32)
    if deep > here:
        seed = jnp.concatenate([seed, jnp.zeros((deep - here, features), F32)], axis=0)
    for d in range(devices):
        seed_ref[d] = seed


def split_columns(initial, conductivity, step_count, emit_steps, inputs, blocks, devices):
    _, rows, total = initial.shape
    width = tiles_for(total // blocks) * LANES
    here, features = inputs.shape
    return pl.pallas_call(
        split_kernel,
        in_specs=[scalars, scalars, far, far, far],
        out_specs=[whole, whole],
        out_shape=[
            jax.ShapeDtypeStruct((blocks, 2, rows, width), F32),
            jax.ShapeDtypeStruct((devices, -(-here // 8) * 8, features), F32),
        ],
        scratch_shapes=[
            pltpu.VMEM(initial.shape, F32),
            pltpu.VMEM(conductivity.shape, F32),
            pltpu.VMEM(inputs.shape, BF16),
            pltpu.SemaphoreType.DMA((3,)),
        ],
        compiler_params=params(),
    )(step_count, emit_steps, initial, conductivity, inputs)


def advance(state, rate, history, pitch, part, fields, now, t):
    _, _, tiles, depth, _ = state.shape
    rows = (depth - 16) // 3
    later = 1 - now
    for tile in range(part, 3 * rows // 8 - part):
        a = 8 + 8 * tile
        for f in fields:
            middle = [state[f, now, j, a : a + 8, :] for j in range(tiles)]
            west = [pltpu.roll(middle[-1], 1, 1)] + middle[:-1]
            east = middle[1:] + [pltpu.roll(middle[0], LANES - 1, 1)]
            for j in range(tiles):
                north = state[f, now, j, a - 1 : a + 7, :]
                south = state[f, now, j, a + 1 : a + 9, :]
                beside = (north + south) + (west[j] + east[j])
                gain = rate[f, j, a : a + 8, :] * (1.0 + 0.25 * jnp.tanh(middle[j]))
                value = middle[j] + gain * (beside - 4.0 * middle[j])
                state[f, later, j, a : a + 8, :] = value
                if rows <= 8 * tile < 2 * rows:
                    start = (8 * tile - rows) * pitch + f * STEPS + t
                    history[j, pl.ds(start, 8, stride=pitch), :] = value


def fold_rows(value, out_ref):
    devices, deep, folded = out_ref.shape
    batch, units = value.shape
    here = batch // devices
    for d in range(devices):
        for k in range(units // folded):
            out_ref[d, k * here : (k + 1) * here, :] = value[
                d * here : (d + 1) * here, k * folded : (k + 1) * folded
            ]


def by_row_kernel(first, weight_far, out_far, weight, by_rows, arrived, left):
    pieces, units, rows, cols = weight.shape
    places = [slice(i * units, (i + 1) * units) for i in range(pieces)]
    sources = [slice(first + i * units, first + (i + 1) * units) for i in range(pieces)]
    loads = [
        pltpu.make_async_copy(weight_far.at[sources[i]], weight.at[i], arrived.at[i])
        for i in range(pieces)
    ]
    stores = [
        pltpu.make_async_copy(by_rows.at[i], out_far.at[:, places[i], :], left.at[i])
        for i in range(pieces)
    ]
    for load in loads:
        load.start()
    for i in range(pieces):
        loads[i].wait()

        def some_units(u, _):
            place = pl.ds(pl.multiple_of(u * 16, 16), 16)
            for c in range(cols // LANES):
                for r in range(0, rows, 16):
                    block = weight[i, place, r : r + 16, lane_tile(c)]
                    by_rows[i, r : r + 16, place, lane_tile(c)] = jnp.swapaxes(block, 0, 1)
            return 0

        lax.fori_loop(0, units // 16, some_units, 0)
        stores[i].start()
    for store in stores:
        store.wait()


def by_row(weight, half, pieces=4):
    units, rows, cols = weight.shape
    units = units // 2
    return pl.pallas_call(
        functools.partial(by_row_kernel, half * units),
        in_specs=[far],
        out_specs=far,
        out_shape=jax.ShapeDtypeStruct((rows, units, cols), BF16),
        scratch_shapes=[
            pltpu.VMEM((pieces, units // pieces, rows, cols), BF16),
            pltpu.VMEM((pieces, rows, units // pieces, cols), BF16),
            pltpu.SemaphoreType.DMA((pieces,)),
            pltpu.SemaphoreType.DMA((pieces,)),
        ],
        compiler_params=params(),
        cost_estimate=pl.CostEstimate(
            flops=0, bytes_accessed=4 * units * rows * cols, transcendentals=0
        ),
    )(weight)


def forward(seed_ref, first_ref, second_ref, third_ref, inputs, act_a, act_b, hidden, gate, raw):
    devices = seed_ref.shape[0]
    here = inputs.shape[0] // devices
    for d in range(devices):
        raw[d * here : (d + 1) * here, :] = seed_ref[d, :here, :]
    inputs[...] = raw[...].astype(BF16)
    act = jnp.tanh(dot(inputs[...], first_ref[...]))
    act_a[...] = act
    act = jnp.tanh(dot(act.astype(BF16), second_ref[...]))
    act_b[...] = act
    act = jnp.tanh(dot(act.astype(BF16), third_ref[...]))
    hidden[...] = act.astype(BF16)
    gate[...] = 1.0 - act * act


def main_kernel(
    scale, snaps, own_far, top_far, bottom_far, seed_far, low_far, high_far, assign_far, first_far, second_far, third_far,
    res_far, back_ref, in_far, a_far, b_far, hid_far,
    state, rate, history, picked, predicted, by_rows, total, raw, assigned, first, second, third,
    own_ref, top_ref, bottom_ref, seed_ref, gather, gate, res, inputs, act_a, act_b, hidden, arrived, filled, left,
):
    fields, _, rows, width = own_ref.shape
    _, batch, cols = predicted.shape
    units = by_rows.shape[1]
    tiles = width // LANES
    entries = fields * STEPS
    pitch = entries + 1
    pairs = (
        (top_far, top_ref), (own_far, own_ref), (bottom_far, bottom_ref),
        (seed_far, seed_ref), (first_far, first), (second_far, second), (third_far, third), (assign_far, assigned),
    )
    loads = [
        pltpu.make_async_copy(source, target, arrived.at[i])
        for i, (source, target) in enumerate(pairs)
    ]
    for load in loads:
        load.start()
    together = 2 if fields % 2 == 0 else 1
    parts = STEPS // 8
    turns = fields // together * parts
    fills = [
        [
            pltpu.make_async_copy(
                source.at[low : low + 4],
                by_rows.at[low : low + 4, half * units // 2 : (half + 1) * units // 2, :],
                filled.at[half, low // 4],
            )
            for half, source in enumerate((low_far, high_far))
        ]
        for low in range(0, rows, 4)
    ]
    place = lax.broadcasted_iota(jnp.int32, (width, cols), 0)
    column = lax.broadcasted_iota(jnp.int32, (width, cols), 1) + STEPS
    gather[...] = (tiles * (place % LANES) + place // LANES == column).astype(F32).astype(BF16)
    for load in loads[:3]:
        load.wait()
    for pair in fills:
        for fill in pair:
            fill.start()

    for f in range(fields):
        for now in range(2):
            for j in range(tiles):
                state[f, now, j, :8, :] = jnp.zeros((8, LANES), F32)
                state[f, now, j, 8 + 3 * rows :, :] = jnp.zeros((8, LANES), F32)
        for j in range(tiles):
            for place, ref in enumerate((top_ref, own_ref, bottom_ref)):
                low = 8 + place * rows
                state[f, 0, j, low : low + rows, :] = ref[f, 0, :, lane_tile(j)]
                rate[f, j, low : low + rows, :] = ref[f, 1, :, lane_tile(j)]
                if place != 1:
                    state[f, 1, j, low : low + rows, :] = ref[f, 0, :, lane_tile(j)]
    def solve(turn, first_row):
        which = [turn // parts * together + i for i in range(together)]
        part = turn % parts

        def two_steps(pair, _):
            for now in range(2):
                advance(state, rate, history, pitch, part, which, now, 2 * pair + now)
            if first_row is not None:
                r = first_row + pair - 4 * part
                predicted[r] = dot(hidden[...], by_rows[r])
            return 0

        lax.fori_loop(4 * part, 4 * part + 4, two_steps, 0)

    solve(0, None)
    for load in loads[3:]:
        load.wait()
    forward(seed_ref, first, second, third, inputs, act_a, act_b, hidden, gate, raw)
    stores = [
        pltpu.make_async_copy(source, target, left.at[i])
        for i, (source, target) in enumerate(
            ((inputs, in_far), (act_a, a_far), (act_b, b_far), (hidden, hid_far))
        )
    ]
    for store in stores:
        store.start()
    for turn in range(1, turns):
        if turn <= len(fills):
            for fill in fills[turn - 1]:
                fill.wait()
        solve(turn, 4 * (turn - 1) if turn <= len(fills) else None)
    for turn in range(turns, len(fills) + 1):
        for fill in fills[turn - 1]:
            fill.wait()
        for r in range(4 * (turn - 1), 4 * turn):
            predicted[r] = dot(hidden[...], by_rows[r])

    lane = lax.broadcasted_iota(jnp.int32, (snaps, entries), 1)
    steps = []
    for f in range(fields):
        last = own_ref[f, 0, :snaps, META : META + 1].astype(jnp.int32)
        steps.append((lane == f * STEPS + last).astype(F32))
    steps = jnp.concatenate(steps, axis=0).astype(BF16)
    number = lax.broadcasted_iota(jnp.int32, (fields * snaps, batch), 0)
    chosen = (number == assigned[...]).astype(F32).astype(BF16)
    hot = contract_rows(chosen, steps).astype(BF16)
    chunk = 8
    for i in range(rows // chunk):
        for k in range(chunk):
            low = (i * chunk + k) * pitch
            for j in range(tiles):
                states = history[j, low : low + entries, :].astype(BF16)
                picked[i % 2, k * batch : (k + 1) * batch, lane_tile(j)] = dot(hot, states).astype(BF16)
        targets = dot(picked[i % 2], gather[...])
        for k in range(chunk):
            r = i * chunk + k
            residual = ((predicted[r] - targets[k * batch : (k + 1) * batch]) * scale).astype(BF16)
            res[r] = residual
            part = contract_cols(residual, by_rows[r])
            back = part if k == 0 else back + part
        total[...] = back if i == 0 else total[...] + back
        place = slice(i * chunk, (i + 1) * chunk)
        stores.append(pltpu.make_async_copy(res.at[place], res_far.at[place], left.at[4 + i]))
        stores[-1].start()
    total[...] = total[...] * gate[...]
    fold_rows(total, back_ref)
    for store in stores:
        store.wait()


def main(assign, own, top, bottom, seeds, w_first, w_second, w_third, halves, snaps, here, fold):
    rows, units, cols = halves[0].shape
    units = 2 * units
    features = w_first.shape[0]
    devices = seeds.shape[0]
    batch = devices * here
    fields, _, _, width = own.shape
    tiles = width // LANES
    depth = 3 * rows + 16
    entries = fields * STEPS
    scale = 1.0 / float(batch) ** 0.5
    folded = (devices, here * fold, units // fold)
    kept = [
        ((rows, batch, cols), BF16),
        ((batch, features), BF16),
        ((batch, units), F32),
        ((batch, units), F32),
        ((batch, units), BF16),
    ]
    shapes = [jax.ShapeDtypeStruct(*k) for k in kept]
    return pl.pallas_call(
        functools.partial(main_kernel, scale, snaps),
        in_specs=[far] * 10,
        out_specs=[far, whole] + [far] * 4,
        out_shape=[shapes[0], jax.ShapeDtypeStruct(folded, F32)] + shapes[1:],
        scratch_shapes=[
            pltpu.VMEM((fields, 2, tiles, depth, LANES), F32),
            pltpu.VMEM((fields, tiles, depth, LANES), F32),
            pltpu.VMEM((tiles, rows * (entries + 1), LANES), F32),
            pltpu.VMEM((2, 8 * batch, width), BF16),
            pltpu.VMEM((rows, batch, cols), F32),
            pltpu.VMEM((rows, units, cols), BF16),
            pltpu.VMEM((batch, units), F32),
            pltpu.VMEM((batch, features), F32),
            pltpu.VMEM((1, batch), jnp.int32),
            pltpu.VMEM(w_first.shape, BF16),
            pltpu.VMEM(w_second.shape, BF16),
            pltpu.VMEM(w_third.shape, BF16),
            pltpu.VMEM(own.shape, F32),
            pltpu.VMEM(own.shape, F32),
            pltpu.VMEM(own.shape, F32),
            pltpu.VMEM(seeds.shape, F32),
            pltpu.VMEM((width, cols), BF16),
            pltpu.VMEM((batch, units), F32),
        ]
        + [pltpu.VMEM(*k) for k in kept]
        + [
            pltpu.SemaphoreType.DMA((8,)),
            pltpu.SemaphoreType.DMA((2, rows // 4)),
            pltpu.SemaphoreType.DMA((4 + rows // 8,)),
        ],
        compiler_params=params(),
    )(own, top, bottom, seeds, *halves, assign.reshape(1, batch), w_first, w_second, w_third)


def outer_kernel(hid_ref, res_ref, out_ref, grads):
    rows, _, cols = res_ref.shape
    units = out_ref.shape[0]
    for r in range(rows):
        grads[r] = contract_rows(hid_ref[...], res_ref[r]).astype(BF16)
    for c in range(cols // LANES):
        for u in range(0, units, 16):
            for r in range(0, rows, 16):
                block = grads[r : r + 16, u : u + 16, lane_tile(c)]
                out_ref[u : u + 16, r : r + 16, lane_tile(c)] = jnp.swapaxes(block, 0, 1)


def outer(hidden, res, chunk=128):
    rows, batch, cols = res.shape
    units = hidden.shape[1]
    return pl.pallas_call(
        outer_kernel,
        grid=(units // chunk,),
        in_specs=[
            pl.BlockSpec((batch, chunk), lambda i: (0, i)),
            pl.BlockSpec((rows, batch, cols), lambda i: (0, 0, 0)),
        ],
        out_specs=pl.BlockSpec((chunk, rows, cols), lambda i: (i, 0, 0)),
        out_shape=jax.ShapeDtypeStruct((units, rows, cols), BF16),
        scratch_shapes=[pltpu.VMEM((rows, chunk, cols), BF16)],
        compiler_params=params(),
        cost_estimate=pl.CostEstimate(
            flops=2 * batch * units * rows * cols,
            bytes_accessed=4 * units * rows * cols,
            transcendentals=0,
        ),
    )(hidden, res)


def delta_kernel(pieces, out_ref):
    devices = pieces.shape[0]
    delta = [pieces[d] for d in range(devices)]
    while len(delta) > 1:
        delta = [a + b for a, b in zip(delta[::2], delta[1::2])] + delta[len(delta) // 2 * 2 :]
    delta = delta[0].astype(BF16)
    for d in range(devices):
        out_ref[d] = delta


def delta_spread(pieces):
    return pl.pallas_call(
        delta_kernel,
        in_specs=[whole],
        out_specs=whole,
        out_shape=jax.ShapeDtypeStruct(pieces.shape, BF16),
        compiler_params=params(16384),
    )(pieces)


def backward_kernel(
    inputs_far, a_far, b_far, delta_far, second_far, third_far, g1_far, g2_far, g3_far,
    inputs, act_a, act_b, folded, second, third, wide, unfolded, g1, g2, g3, arrived, left,
):
    pairs = (
        (delta_far, folded), (b_far, act_b), (third_far, third),
        (a_far, act_a), (second_far, second), (inputs_far, inputs),
    )
    loads = [
        pltpu.make_async_copy(source, target, arrived.at[i])
        for i, (source, target) in enumerate(pairs)
    ]
    for load in loads:
        load.start()
    stores = [
        pltpu.make_async_copy(source, target, left.at[i])
        for i, (source, target) in enumerate(((g3, g3_far), (g2, g2_far), (g1, g1_far)))
    ]
    devices, deep, width = folded.shape
    batch, units = act_a.shape
    here = batch // devices
    loads[0].wait()
    wide[...] = folded[...].astype(F32)
    for d in range(devices):
        for k in range(units // width):
            unfolded[d * here : (d + 1) * here, k * width : (k + 1) * width] = wide[
                d, k * here : (k + 1) * here, :
            ]
    delta = unfolded[...].astype(BF16)
    loads[1].wait()
    act = act_b[...]
    g3[...] = contract_rows(act.astype(BF16), delta)
    stores[0].start()
    loads[2].wait()
    delta = (contract_cols(delta, third[...]) * (1.0 - act * act)).astype(BF16)
    loads[3].wait()
    act = act_a[...]
    g2[...] = contract_rows(act.astype(BF16), delta)
    stores[1].start()
    loads[4].wait()
    delta = (contract_cols(delta, second[...]) * (1.0 - act * act)).astype(BF16)
    loads[5].wait()
    g1[...] = contract_rows(inputs[...], delta)
    stores[2].start()
    for store in stores:
        store.wait()


def backward(inputs, act_a, act_b, delta, w_second, w_third):
    batch, units = act_a.shape
    shapes = [(inputs.shape[1], units), (units, units), (units, units)]
    return pl.pallas_call(
        backward_kernel,
        in_specs=[far] * 6,
        out_specs=[far] * 3,
        out_shape=[jax.ShapeDtypeStruct(shape, F32) for shape in shapes],
        scratch_shapes=[
            pltpu.VMEM(inputs.shape, BF16),
            pltpu.VMEM(act_a.shape, F32),
            pltpu.VMEM(act_b.shape, F32),
            pltpu.VMEM(delta.shape, BF16),
            pltpu.VMEM(w_second.shape, BF16),
            pltpu.VMEM(w_third.shape, BF16),
            pltpu.VMEM(delta.shape, F32),
            pltpu.VMEM((batch, units), F32),
        ]
        + [pltpu.VMEM(shape, F32) for shape in shapes]
        + [pltpu.SemaphoreType.DMA((6,)), pltpu.SemaphoreType.DMA((3,))],
        compiler_params=params(),
    )(inputs, act_a, act_b, delta, w_second, w_third)


def swap(value, axes):
    return lax.all_to_all(value, axes, split_axis=0, concat_axis=0, tiled=True)


def per_device(
    initial,
    conductivity,
    step_count,
    emit_steps,
    assign,
    sample_inputs,
    w_first,
    w_second,
    w_third,
    w_out,
):
    groups, strips = lax.axis_size("group"), lax.axis_size("strip")
    devices = groups * strips
    here = sample_inputs.shape[0]
    fold = max(1, 8 // here)
    blocks, seeds = split_columns(
        initial, conductivity, step_count, emit_steps, sample_inputs, groups, devices
    )
    blocks, w_out = lax.optimization_barrier((blocks, w_out))
    own = swap(blocks, "group")
    low = by_row(w_out, 0)
    own, low, w_out = lax.optimization_barrier((own, low, w_out))
    down = [(i, i + 1) for i in range(strips - 1)]
    top = lax.ppermute(own, "strip", down)
    bottom = lax.ppermute(own, "strip", [(j, i) for i, j in down])
    own, seeds = lax.optimization_barrier((own, seeds))
    seeds = swap(seeds, ALL)
    res, partial, inputs, act_a, act_b, hidden = main(
        assign, own, top, bottom, seeds, w_first, w_second, w_third, (low, by_row(w_out, 1)),
        emit_steps.shape[1], here, fold,
    )
    pieces = swap(partial, ALL)
    grad_out = outer(hidden, res)
    pieces, grad_out = lax.optimization_barrier((pieces, grad_out))
    delta = swap(delta_spread(pieces), ALL)
    grads = backward(inputs, act_a, act_b, delta, w_second, w_third)
    return (*grads, grad_out)


def solution(mesh):
    placed = (
        P("group", "strip", None),
        P("group", "strip", None),
        P("group"),
        P("group", None),
        P(),
        P(("group", "strip"), None),
        P(),
        P(),
        P(),
        P(None, "strip", "group"),
    )
    return jax.shard_map(
        per_device,
        mesh=mesh,
        in_specs=placed,
        out_specs=(P(), P(), P(), P(None, "strip", "group")),
        check_vma=False,
    )
```

```python
import functools

import jax
import jax.numpy as jnp
from jax import lax
from jax.experimental import pallas as pl
from jax.experimental.pallas import tpu as pltpu
from jax.sharding import PartitionSpec as P

STEPS = 32
LANES = 128
META = 120
step_rate = 0.125

BF16 = jnp.bfloat16
F32 = jnp.float32
ALL = ("group", "strip")
whole = pl.BlockSpec(memory_space=pltpu.VMEM)
scalars = pl.BlockSpec(memory_space=pltpu.SMEM)
far = pl.BlockSpec(memory_space=pl.ANY)


def params(kibibytes=65024):
    return pltpu.CompilerParams(vmem_limit_bytes=kibibytes << 10)


def dot(left, right):
    return jnp.dot(left, right, preferred_element_type=F32)


def contract_rows(left, right):
    return lax.dot_general(left, right, (((0,), (0,)), ((), ())), preferred_element_type=F32)


def contract_cols(left, right):
    return lax.dot_general(left, right, (((1,), (1,)), ((), ())), preferred_element_type=F32)


def lane_tile(c):
    return slice(c * LANES, (c + 1) * LANES)


def tiles_for(cols):
    return -(-(cols + 2 * STEPS) // LANES)


def split_kernel(
    count_ref, emit_ref, field_far, kappa_far, inputs_far, out_far, seed_far,
    field_ref, kappa_ref, inputs_ref, out_ref, seed_ref, arrived, left,
):
    loads = [
        pltpu.make_async_copy(source, target, arrived.at[i])
        for i, (source, target) in enumerate(
            ((field_far, field_ref), (kappa_far, kappa_ref), (inputs_far, inputs_ref))
        )
    ]
    for load in loads:
        load.start()
    blocks, _, rows, width = out_ref.shape
    tiles = width // LANES
    total = field_ref.shape[2]
    cols = total // blocks
    span = cols + 2 * LANES
    source = lax.broadcasted_iota(jnp.int32, (span, width), 0) - (LANES - STEPS)
    place = lax.broadcasted_iota(jnp.int32, (span, width), 1)
    wanted = tiles * (place % LANES) + place // LANES
    deal = ((source == wanted) & (wanted < cols + 2 * STEPS)).astype(F32).astype(BF16)
    stores = [pltpu.make_async_copy(seed_ref, seed_far, left.at[blocks])]
    loads[2].wait()
    here = inputs_ref.shape[0]
    devices, deep, features = seed_ref.shape
    seed = inputs_ref[...].astype(F32)
    if deep > here:
        seed = jnp.concatenate([seed, jnp.zeros((deep - here, features), F32)], axis=0)
    for d in range(devices):
        seed_ref[d] = seed
    stores[0].start()
    for load in loads[:2]:
        load.wait()
    none = jnp.zeros((2 * rows, LANES), F32)
    both = jnp.concatenate([field_ref[0], kappa_ref[0] * step_rate], axis=0)
    both = jnp.concatenate([none, both, none], axis=1)
    high = both.astype(BF16)
    rest = both - high.astype(F32)
    middle = rest.astype(BF16)
    low = (rest - middle.astype(F32)).astype(BF16)
    lane = lax.broadcasted_iota(jnp.int32, (rows, LANES), 1)
    row = lax.broadcasted_iota(jnp.int32, (rows, LANES), 0)
    meta = jnp.zeros((rows, LANES), F32)
    for s in range(emit_ref.shape[1]):
        last = jnp.minimum(emit_ref[0, s], count_ref[0]) - 1
        meta = jnp.where(row == s, last.astype(F32), meta)
    windows = [slice(g * cols, g * cols + span) for g in range(blocks)]
    stacked = [part[:, window] for window in windows for part in (high, middle, low)]
    product = dot(jnp.concatenate(stacked, axis=0), deal)
    for g in range(blocks):
        parts = [product[2 * rows * (3 * g + i) : 2 * rows * (3 * g + i + 1)] for i in range(3)]
        dealt = parts[0] + parts[1] + parts[2]
        out_ref[g, 0] = dealt[:rows]
        out_ref[g, 1] = dealt[rows:]
        out_ref[g, 0, :, :LANES] = jnp.where(lane == META, meta, dealt[:rows, :LANES])
        stores.append(pltpu.make_async_copy(out_ref.at[g], out_far.at[g], left.at[g]))
        stores[-1].start()
    for store in stores:
        store.wait()


def split_columns(initial, conductivity, step_count, emit_steps, inputs, blocks, devices):
    _, rows, total = initial.shape
    width = tiles_for(total // blocks) * LANES
    here, features = inputs.shape
    return pl.pallas_call(
        split_kernel,
        in_specs=[scalars, scalars, far, far, far],
        out_specs=[far, far],
        out_shape=[
            jax.ShapeDtypeStruct((blocks, 2, rows, width), F32),
            jax.ShapeDtypeStruct((devices, -(-here // 8) * 8, features), F32),
        ],
        scratch_shapes=[
            pltpu.VMEM(initial.shape, F32),
            pltpu.VMEM(conductivity.shape, F32),
            pltpu.VMEM(inputs.shape, BF16),
            pltpu.VMEM((blocks, 2, rows, width), F32),
            pltpu.VMEM((devices, -(-here // 8) * 8, features), F32),
            pltpu.SemaphoreType.DMA((3,)),
            pltpu.SemaphoreType.DMA((blocks + 1,)),
        ],
        compiler_params=params(),
    )(step_count, emit_steps, initial, conductivity, inputs)


def advance(state, rate, history, pitch, part, fields, now, t):
    _, _, tiles, depth, _ = state.shape
    rows = (depth - 16) // 3
    later = 1 - now
    for tile in range(part, 3 * rows // 8 - part):
        a = 8 + 8 * tile
        for f in fields:
            middle = [state[f, now, j, a : a + 8, :] for j in range(tiles)]
            west = [pltpu.roll(middle[-1], 1, 1)] + middle[:-1]
            east = middle[1:] + [pltpu.roll(middle[0], LANES - 1, 1)]
            for j in range(tiles):
                north = state[f, now, j, a - 1 : a + 7, :]
                south = state[f, now, j, a + 1 : a + 9, :]
                beside = (north + south) + (west[j] + east[j])
                gain = rate[f, j, a : a + 8, :] * (1.0 + 0.25 * jnp.tanh(middle[j]))
                value = middle[j] + gain * (beside - 4.0 * middle[j])
                state[f, later, j, a : a + 8, :] = value
                if rows <= 8 * tile < 2 * rows:
                    start = (8 * tile - rows) * pitch + f * STEPS + t
                    history[j, pl.ds(start, 8, stride=pitch), :] = value


def fold_rows(value, out_ref):
    devices, deep, folded = out_ref.shape
    batch, units = value.shape
    here = batch // devices
    for d in range(devices):
        for k in range(units // folded):
            out_ref[d, k * here : (k + 1) * here, :] = value[
                d * here : (d + 1) * here, k * folded : (k + 1) * folded
            ]


def by_row_kernel(first, weight_far, out_far, weight, by_rows, arrived, left):
    pieces, units, rows, cols = weight.shape
    places = [slice(i * units, (i + 1) * units) for i in range(pieces)]
    sources = [slice(first + i * units, first + (i + 1) * units) for i in range(pieces)]
    loads = [
        pltpu.make_async_copy(weight_far.at[sources[i]], weight.at[i], arrived.at[i])
        for i in range(pieces)
    ]
    stores = [
        pltpu.make_async_copy(by_rows.at[i], out_far.at[:, places[i], :], left.at[i])
        for i in range(pieces)
    ]
    for load in loads:
        load.start()
    for i in range(pieces):
        loads[i].wait()

        def some_units(u, _):
            place = pl.ds(pl.multiple_of(u * 16, 16), 16)
            for c in range(cols // LANES):
                for r in range(0, rows, 16):
                    block = weight[i, place, r : r + 16, lane_tile(c)]
                    by_rows[i, r : r + 16, place, lane_tile(c)] = jnp.swapaxes(block, 0, 1)
            return 0

        lax.fori_loop(0, units // 16, some_units, 0)
        stores[i].start()
    for store in stores:
        store.wait()


def by_row(weight, half, pieces=4):
    units, rows, cols = weight.shape
    units = units // 2
    return pl.pallas_call(
        functools.partial(by_row_kernel, half * units),
        in_specs=[far],
        out_specs=far,
        out_shape=jax.ShapeDtypeStruct((rows, units, cols), BF16),
        scratch_shapes=[
            pltpu.VMEM((pieces, units // pieces, rows, cols), BF16),
            pltpu.VMEM((pieces, rows, units // pieces, cols), BF16),
            pltpu.SemaphoreType.DMA((pieces,)),
            pltpu.SemaphoreType.DMA((pieces,)),
        ],
        compiler_params=params(),
        cost_estimate=pl.CostEstimate(
            flops=0, bytes_accessed=4 * units * rows * cols, transcendentals=0
        ),
    )(weight)


def forward(seed_ref, first_ref, second_ref, third_ref, inputs, act_a, act_b, hidden, gate, raw):
    devices = seed_ref.shape[0]
    here = inputs.shape[0] // devices
    for d in range(devices):
        raw[d * here : (d + 1) * here, :] = seed_ref[d, :here, :]
    inputs[...] = raw[...].astype(BF16)
    act = jnp.tanh(dot(inputs[...], first_ref[...]))
    act_a[...] = act
    act = jnp.tanh(dot(act.astype(BF16), second_ref[...]))
    act_b[...] = act
    act = jnp.tanh(dot(act.astype(BF16), third_ref[...]))
    hidden[...] = act.astype(BF16)
    gate[...] = 1.0 - act * act


def main_kernel(
    scale, snaps, own_far, top_far, bottom_far, seed_far, low_far, high_far, assign_far, first_far, second_far, third_far,
    res_far, back_ref, in_far, a_far, b_far, hid_far,
    state, rate, history, picked, predicted, by_rows, total, raw, assigned, first, second, third,
    own_ref, top_ref, bottom_ref, seed_ref, gather, gate, res, inputs, act_a, act_b, hidden, arrived, filled, left,
):
    fields, _, rows, width = own_ref.shape
    _, batch, cols = predicted.shape
    units = by_rows.shape[1]
    tiles = width // LANES
    entries = fields * STEPS
    pitch = entries + 1
    pairs = (
        (top_far, top_ref), (own_far, own_ref), (bottom_far, bottom_ref),
        (seed_far, seed_ref), (first_far, first), (second_far, second), (third_far, third), (assign_far, assigned),
    )
    loads = [
        pltpu.make_async_copy(source, target, arrived.at[i])
        for i, (source, target) in enumerate(pairs)
    ]
    for load in loads:
        load.start()
    together = 2 if fields % 2 == 0 else 1
    parts = STEPS // 8
    turns = fields // together * parts
    fills = [
        [
            pltpu.make_async_copy(
                source.at[low : low + 4],
                by_rows.at[low : low + 4, half * units // 2 : (half + 1) * units // 2, :],
                filled.at[half, low // 4],
            )
            for half, source in enumerate((low_far, high_far))
        ]
        for low in range(0, rows, 4)
    ]
    place = lax.broadcasted_iota(jnp.int32, (width, cols), 0)
    column = lax.broadcasted_iota(jnp.int32, (width, cols), 1) + STEPS
    gather[...] = (tiles * (place % LANES) + place // LANES == column).astype(F32).astype(BF16)
    for load in loads[:3]:
        load.wait()
    for pair in fills:
        for fill in pair:
            fill.start()

    for f in range(fields):
        for now in range(2):
            for j in range(tiles):
                state[f, now, j, :8, :] = jnp.zeros((8, LANES), F32)
                state[f, now, j, 8 + 3 * rows :, :] = jnp.zeros((8, LANES), F32)
        for j in range(tiles):
            for place, ref in enumerate((top_ref, own_ref, bottom_ref)):
                low = 8 + place * rows
                state[f, 0, j, low : low + rows, :] = ref[f, 0, :, lane_tile(j)]
                rate[f, j, low : low + rows, :] = ref[f, 1, :, lane_tile(j)]
                if place != 1:
                    state[f, 1, j, low : low + rows, :] = ref[f, 0, :, lane_tile(j)]
    def solve(turn, first_row):
        which = [turn // parts * together + i for i in range(together)]
        part = turn % parts

        def two_steps(pair, _):
            for now in range(2):
                advance(state, rate, history, pitch, part, which, now, 2 * pair + now)
            if first_row is not None:
                r = first_row + pair - 4 * part
                predicted[r] = dot(hidden[...], by_rows[r])
            return 0

        lax.fori_loop(4 * part, 4 * part + 4, two_steps, 0)

    which = list(range(together))
    for t in range(4):
        advance(state, rate, history, pitch, 0, which, t % 2, t)
    for load in loads[3:]:
        load.wait()
    forward(seed_ref, first, second, third, inputs, act_a, act_b, hidden, gate, raw)
    for t in range(4, 8):
        advance(state, rate, history, pitch, 0, which, t % 2, t)
    stores = [
        pltpu.make_async_copy(source, target, left.at[i])
        for i, (source, target) in enumerate(
            ((inputs, in_far), (act_a, a_far), (act_b, b_far), (hidden, hid_far))
        )
    ]
    for store in stores:
        store.start()
    for turn in range(1, turns):
        if turn <= len(fills):
            for fill in fills[turn - 1]:
                fill.wait()
        solve(turn, 4 * (turn - 1) if turn <= len(fills) else None)
    for turn in range(turns, len(fills) + 1):
        for fill in fills[turn - 1]:
            fill.wait()
        for r in range(4 * (turn - 1), 4 * turn):
            predicted[r] = dot(hidden[...], by_rows[r])

    lane = lax.broadcasted_iota(jnp.int32, (snaps, entries), 1)
    steps = []
    for f in range(fields):
        last = own_ref[f, 0, :snaps, META : META + 1].astype(jnp.int32)
        steps.append((lane == f * STEPS + last).astype(F32))
    steps = jnp.concatenate(steps, axis=0).astype(BF16)
    number = lax.broadcasted_iota(jnp.int32, (fields * snaps, batch), 0)
    chosen = (number == assigned[...]).astype(F32).astype(BF16)
    hot = contract_rows(chosen, steps).astype(BF16)
    chunk = 8
    for i in range(rows // chunk):
        for k in range(chunk):
            low = (i * chunk + k) * pitch
            for j in range(tiles):
                states = history[j, low : low + entries, :].astype(BF16)
                picked[i % 2, k * batch : (k + 1) * batch, lane_tile(j)] = dot(hot, states).astype(BF16)
        targets = dot(picked[i % 2], gather[...])
        for k in range(chunk):
            r = i * chunk + k
            residual = ((predicted[r] - targets[k * batch : (k + 1) * batch]) * scale).astype(BF16)
            res[r] = residual
            part = contract_cols(residual, by_rows[r])
            back = part if k == 0 else back + part
        total[...] = back if i == 0 else total[...] + back
        place = slice(i * chunk, (i + 1) * chunk)
        stores.append(pltpu.make_async_copy(res.at[place], res_far.at[place], left.at[4 + i]))
        stores[-1].start()
    total[...] = total[...] * gate[...]
    fold_rows(total, back_ref)
    for store in stores:
        store.wait()


def main(assign, own, top, bottom, seeds, w_first, w_second, w_third, halves, snaps, here, fold):
    rows, units, cols = halves[0].shape
    units = 2 * units
    features = w_first.shape[0]
    devices = seeds.shape[0]
    batch = devices * here
    fields, _, _, width = own.shape
    tiles = width // LANES
    depth = 3 * rows + 16
    entries = fields * STEPS
    scale = 1.0 / float(batch) ** 0.5
    folded = (devices, here * fold, units // fold)
    kept = [
        ((rows, batch, cols), BF16),
        ((batch, features), BF16),
        ((batch, units), F32),
        ((batch, units), F32),
        ((batch, units), BF16),
    ]
    shapes = [jax.ShapeDtypeStruct(*k) for k in kept]
    return pl.pallas_call(
        functools.partial(main_kernel, scale, snaps),
        in_specs=[far] * 10,
        out_specs=[far, whole] + [far] * 4,
        out_shape=[shapes[0], jax.ShapeDtypeStruct(folded, F32)] + shapes[1:],
        scratch_shapes=[
            pltpu.VMEM((fields, 2, tiles, depth, LANES), F32),
            pltpu.VMEM((fields, tiles, depth, LANES), F32),
            pltpu.VMEM((tiles, rows * (entries + 1), LANES), F32),
            pltpu.VMEM((2, 8 * batch, width), BF16),
            pltpu.VMEM((rows, batch, cols), F32),
            pltpu.VMEM((rows, units, cols), BF16),
            pltpu.VMEM((batch, units), F32),
            pltpu.VMEM((batch, features), F32),
            pltpu.VMEM((1, batch), jnp.int32),
            pltpu.VMEM(w_first.shape, BF16),
            pltpu.VMEM(w_second.shape, BF16),
            pltpu.VMEM(w_third.shape, BF16),
            pltpu.VMEM(own.shape, F32),
            pltpu.VMEM(own.shape, F32),
            pltpu.VMEM(own.shape, F32),
            pltpu.VMEM(seeds.shape, F32),
            pltpu.VMEM((width, cols), BF16),
            pltpu.VMEM((batch, units), F32),
        ]
        + [pltpu.VMEM(*k) for k in kept]
        + [
            pltpu.SemaphoreType.DMA((8,)),
            pltpu.SemaphoreType.DMA((2, rows // 4)),
            pltpu.SemaphoreType.DMA((4 + rows // 8,)),
        ],
        compiler_params=params(),
    )(own, top, bottom, seeds, *halves, assign.reshape(1, batch), w_first, w_second, w_third)


def outer_kernel(hid_ref, res_ref, out_ref, grads):
    rows, _, cols = res_ref.shape
    units = out_ref.shape[0]
    for r in range(rows):
        grads[r] = contract_rows(hid_ref[...], res_ref[r]).astype(BF16)
    for c in range(cols // LANES):
        for u in range(0, units, 16):
            for r in range(0, rows, 16):
                block = grads[r : r + 16, u : u + 16, lane_tile(c)]
                out_ref[u : u + 16, r : r + 16, lane_tile(c)] = jnp.swapaxes(block, 0, 1)


def outer(hidden, res, chunk=128):
    rows, batch, cols = res.shape
    units = hidden.shape[1]
    return pl.pallas_call(
        outer_kernel,
        grid=(units // chunk,),
        in_specs=[
            pl.BlockSpec((batch, chunk), lambda i: (0, i)),
            pl.BlockSpec((rows, batch, cols), lambda i: (0, 0, 0)),
        ],
        out_specs=pl.BlockSpec((chunk, rows, cols), lambda i: (i, 0, 0)),
        out_shape=jax.ShapeDtypeStruct((units, rows, cols), BF16),
        scratch_shapes=[pltpu.VMEM((rows, chunk, cols), BF16)],
        compiler_params=params(),
        cost_estimate=pl.CostEstimate(
            flops=2 * batch * units * rows * cols,
            bytes_accessed=4 * units * rows * cols,
            transcendentals=0,
        ),
    )(hidden, res)


def delta_kernel(pieces, out_ref):
    devices = pieces.shape[0]
    delta = [pieces[d] for d in range(devices)]
    while len(delta) > 1:
        delta = [a + b for a, b in zip(delta[::2], delta[1::2])] + delta[len(delta) // 2 * 2 :]
    delta = delta[0].astype(BF16)
    for d in range(devices):
        out_ref[d] = delta


def delta_spread(pieces):
    return pl.pallas_call(
        delta_kernel,
        in_specs=[whole],
        out_specs=whole,
        out_shape=jax.ShapeDtypeStruct(pieces.shape, BF16),
        compiler_params=params(16384),
    )(pieces)


def backward_kernel(
    inputs_far, a_far, b_far, delta_far, second_far, third_far, g1_far, g2_far, g3_far,
    inputs, act_a, act_b, folded, second, third, wide, unfolded, g1, g2, g3, arrived, left,
):
    pairs = (
        (delta_far, folded), (b_far, act_b), (third_far, third),
        (a_far, act_a), (second_far, second), (inputs_far, inputs),
    )
    loads = [
        pltpu.make_async_copy(source, target, arrived.at[i])
        for i, (source, target) in enumerate(pairs)
    ]
    for load in loads:
        load.start()
    stores = [
        pltpu.make_async_copy(source, target, left.at[i])
        for i, (source, target) in enumerate(((g3, g3_far), (g2, g2_far), (g1, g1_far)))
    ]
    devices, deep, width = folded.shape
    batch, units = act_a.shape
    here = batch // devices
    loads[0].wait()
    wide[...] = folded[...].astype(F32)
    for d in range(devices):
        for k in range(units // width):
            unfolded[d * here : (d + 1) * here, k * width : (k + 1) * width] = wide[
                d, k * here : (k + 1) * here, :
            ]
    delta = unfolded[...].astype(BF16)
    loads[1].wait()
    act = act_b[...]
    g3[...] = contract_rows(act.astype(BF16), delta)
    stores[0].start()
    loads[2].wait()
    delta = (contract_cols(delta, third[...]) * (1.0 - act * act)).astype(BF16)
    loads[3].wait()
    act = act_a[...]
    g2[...] = contract_rows(act.astype(BF16), delta)
    stores[1].start()
    loads[4].wait()
    delta = (contract_cols(delta, second[...]) * (1.0 - act * act)).astype(BF16)
    loads[5].wait()
    g1[...] = contract_rows(inputs[...], delta)
    stores[2].start()
    for store in stores:
        store.wait()


def backward(inputs, act_a, act_b, delta, w_second, w_third):
    batch, units = act_a.shape
    shapes = [(inputs.shape[1], units), (units, units), (units, units)]
    return pl.pallas_call(
        backward_kernel,
        in_specs=[far] * 6,
        out_specs=[far] * 3,
        out_shape=[jax.ShapeDtypeStruct(shape, F32) for shape in shapes],
        scratch_shapes=[
            pltpu.VMEM(inputs.shape, BF16),
            pltpu.VMEM(act_a.shape, F32),
            pltpu.VMEM(act_b.shape, F32),
            pltpu.VMEM(delta.shape, BF16),
            pltpu.VMEM(w_second.shape, BF16),
            pltpu.VMEM(w_third.shape, BF16),
            pltpu.VMEM(delta.shape, F32),
            pltpu.VMEM((batch, units), F32),
        ]
        + [pltpu.VMEM(shape, F32) for shape in shapes]
        + [pltpu.SemaphoreType.DMA((6,)), pltpu.SemaphoreType.DMA((3,))],
        compiler_params=params(),
    )(inputs, act_a, act_b, delta, w_second, w_third)


def swap(value, axes):
    return lax.all_to_all(value, axes, split_axis=0, concat_axis=0, tiled=True)


def per_device(
    initial,
    conductivity,
    step_count,
    emit_steps,
    assign,
    sample_inputs,
    w_first,
    w_second,
    w_third,
    w_out,
):
    groups, strips = lax.axis_size("group"), lax.axis_size("strip")
    devices = groups * strips
    here = sample_inputs.shape[0]
    fold = max(1, 8 // here)
    blocks, seeds = split_columns(
        initial, conductivity, step_count, emit_steps, sample_inputs, groups, devices
    )
    blocks, w_out = lax.optimization_barrier((blocks, w_out))
    own = swap(blocks, "group")
    low = by_row(w_out, 0)
    own, low, w_out = lax.optimization_barrier((own, low, w_out))
    down = [(i, i + 1) for i in range(strips - 1)]
    top = lax.ppermute(own, "strip", down)
    bottom = lax.ppermute(own, "strip", [(j, i) for i, j in down])
    own, seeds = lax.optimization_barrier((own, seeds))
    seeds = swap(seeds, ALL)
    res, partial, inputs, act_a, act_b, hidden = main(
        assign, own, top, bottom, seeds, w_first, w_second, w_third, (low, by_row(w_out, 1)),
        emit_steps.shape[1], here, fold,
    )
    pieces = swap(partial, ALL)
    grad_out = outer(hidden, res)
    pieces, grad_out = lax.optimization_barrier((pieces, grad_out))
    delta = swap(delta_spread(pieces), ALL)
    grads = backward(inputs, act_a, act_b, delta, w_second, w_third)
    return (*grads, grad_out)


def solution(mesh):
    placed = (
        P("group", "strip", None),
        P("group", "strip", None),
        P("group"),
        P("group", None),
        P(),
        P(("group", "strip"), None),
        P(),
        P(),
        P(),
        P(None, "strip", "group"),
    )
    return jax.shard_map(
        per_device,
        mesh=mesh,
        in_specs=placed,
        out_specs=(P(), P(), P(), P(None, "strip", "group")),
        check_vma=False,
    )
```

```python
import functools

import jax
import jax.numpy as jnp
from jax import lax
from jax.experimental import pallas as pl
from jax.experimental.pallas import tpu as pltpu
from jax.sharding import PartitionSpec as P

STEPS = 32
LANES = 128
META = 120
step_rate = 0.125

BF16 = jnp.bfloat16
F32 = jnp.float32
ALL = ("group", "strip")
whole = pl.BlockSpec(memory_space=pltpu.VMEM)
scalars = pl.BlockSpec(memory_space=pltpu.SMEM)
far = pl.BlockSpec(memory_space=pl.ANY)


def params(kibibytes=65024):
    return pltpu.CompilerParams(vmem_limit_bytes=kibibytes << 10)


def dot(left, right):
    return jnp.dot(left, right, preferred_element_type=F32)


def contract_rows(left, right):
    return lax.dot_general(left, right, (((0,), (0,)), ((), ())), preferred_element_type=F32)


def contract_cols(left, right):
    return lax.dot_general(left, right, (((1,), (1,)), ((), ())), preferred_element_type=F32)


def lane_tile(c):
    return slice(c * LANES, (c + 1) * LANES)


def tiles_for(cols):
    return -(-(cols + 2 * STEPS) // LANES)


def split_kernel(
    count_ref, emit_ref, field_far, kappa_far, inputs_far, out_far, seed_far,
    field_ref, kappa_ref, inputs_ref, out_ref, seed_ref, arrived, left,
):
    loads = [
        pltpu.make_async_copy(source, target, arrived.at[i])
        for i, (source, target) in enumerate(
            ((field_far, field_ref), (kappa_far, kappa_ref), (inputs_far, inputs_ref))
        )
    ]
    for load in loads:
        load.start()
    blocks, _, rows, width = out_ref.shape
    tiles = width // LANES
    total = field_ref.shape[2]
    cols = total // blocks
    span = cols + 2 * LANES
    source = lax.broadcasted_iota(jnp.int32, (span, width), 0) - (LANES - STEPS)
    place = lax.broadcasted_iota(jnp.int32, (span, width), 1)
    wanted = tiles * (place % LANES) + place // LANES
    deal = ((source == wanted) & (wanted < cols + 2 * STEPS)).astype(F32).astype(BF16)
    stores = [pltpu.make_async_copy(seed_ref, seed_far, left.at[blocks])]
    loads[2].wait()
    here = inputs_ref.shape[0]
    devices, deep, features = seed_ref.shape
    seed = inputs_ref[...].astype(F32)
    if deep > here:
        seed = jnp.concatenate([seed, jnp.zeros((deep - here, features), F32)], axis=0)
    for d in range(devices):
        seed_ref[d] = seed
    stores[0].start()
    for load in loads[:2]:
        load.wait()
    none = jnp.zeros((2 * rows, LANES), F32)
    both = jnp.concatenate([field_ref[0], kappa_ref[0] * step_rate], axis=0)
    both = jnp.concatenate([none, both, none], axis=1)
    high = both.astype(BF16)
    rest = both - high.astype(F32)
    middle = rest.astype(BF16)
    low = (rest - middle.astype(F32)).astype(BF16)
    lane = lax.broadcasted_iota(jnp.int32, (rows, LANES), 1)
    row = lax.broadcasted_iota(jnp.int32, (rows, LANES), 0)
    meta = jnp.zeros((rows, LANES), F32)
    for s in range(emit_ref.shape[1]):
        last = jnp.minimum(emit_ref[0, s], count_ref[0]) - 1
        meta = jnp.where(row == s, last.astype(F32), meta)
    windows = [slice(g * cols, g * cols + span) for g in range(blocks)]
    stacked = [part[:, window] for window in windows for part in (high, middle, low)]
    product = dot(jnp.concatenate(stacked, axis=0), deal)
    for g in range(blocks):
        parts = [product[2 * rows * (3 * g + i) : 2 * rows * (3 * g + i + 1)] for i in range(3)]
        dealt = parts[0] + parts[1] + parts[2]
        out_ref[g, 0] = dealt[:rows]
        out_ref[g, 1] = dealt[rows:]
        out_ref[g, 0, :, :LANES] = jnp.where(lane == META, meta, dealt[:rows, :LANES])
        stores.append(pltpu.make_async_copy(out_ref.at[g], out_far.at[g], left.at[g]))
        stores[-1].start()
    for store in stores:
        store.wait()


def split_columns(initial, conductivity, step_count, emit_steps, inputs, blocks, devices):
    _, rows, total = initial.shape
    width = tiles_for(total // blocks) * LANES
    here, features = inputs.shape
    return pl.pallas_call(
        split_kernel,
        in_specs=[scalars, scalars, far, far, far],
        out_specs=[far, far],
        out_shape=[
            jax.ShapeDtypeStruct((blocks, 2, rows, width), F32),
            jax.ShapeDtypeStruct((devices, -(-here // 8) * 8, features), F32),
        ],
        scratch_shapes=[
            pltpu.VMEM(initial.shape, F32),
            pltpu.VMEM(conductivity.shape, F32),
            pltpu.VMEM(inputs.shape, BF16),
            pltpu.VMEM((blocks, 2, rows, width), F32),
            pltpu.VMEM((devices, -(-here // 8) * 8, features), F32),
            pltpu.SemaphoreType.DMA((3,)),
            pltpu.SemaphoreType.DMA((blocks + 1,)),
        ],
        compiler_params=params(),
    )(step_count, emit_steps, initial, conductivity, inputs)


def advance(state, rate, history, pitch, part, fields, now, t):
    _, _, tiles, depth, _ = state.shape
    rows = (depth - 16) // 3
    later = 1 - now
    for tile in range(part, 3 * rows // 8 - part):
        a = 8 + 8 * tile
        for f in fields:
            middle = [state[f, now, j, a : a + 8, :] for j in range(tiles)]
            west = [pltpu.roll(middle[-1], 1, 1)] + middle[:-1]
            east = middle[1:] + [pltpu.roll(middle[0], LANES - 1, 1)]
            for j in range(tiles):
                north = state[f, now, j, a - 1 : a + 7, :]
                south = state[f, now, j, a + 1 : a + 9, :]
                beside = (north + south) + (west[j] + east[j])
                gain = rate[f, j, a : a + 8, :] * (1.0 + 0.25 * jnp.tanh(middle[j]))
                value = middle[j] + gain * (beside - 4.0 * middle[j])
                state[f, later, j, a : a + 8, :] = value
                if rows <= 8 * tile < 2 * rows:
                    start = (8 * tile - rows) * pitch + f * STEPS + t
                    history[j, pl.ds(start, 8, stride=pitch), :] = value


def fold_rows(value, out_ref):
    devices, deep, folded = out_ref.shape
    batch, units = value.shape
    here = batch // devices
    for d in range(devices):
        for k in range(units // folded):
            out_ref[d, k * here : (k + 1) * here, :] = value[
                d * here : (d + 1) * here, k * folded : (k + 1) * folded
            ]


def by_row_kernel(first, weight_far, out_far, weight, by_rows, arrived, left):
    pieces, units, rows, cols = weight.shape
    places = [slice(i * units, (i + 1) * units) for i in range(pieces)]
    sources = [slice(first + i * units, first + (i + 1) * units) for i in range(pieces)]
    loads = [
        pltpu.make_async_copy(weight_far.at[sources[i]], weight.at[i], arrived.at[i])
        for i in range(pieces)
    ]
    stores = [
        pltpu.make_async_copy(by_rows.at[i], out_far.at[:, places[i], :], left.at[i])
        for i in range(pieces)
    ]
    for load in loads:
        load.start()
    for i in range(pieces):
        loads[i].wait()

        def some_units(u, _):
            place = pl.ds(pl.multiple_of(u * 16, 16), 16)
            for c in range(cols // LANES):
                for r in range(0, rows, 16):
                    block = weight[i, place, r : r + 16, lane_tile(c)]
                    by_rows[i, r : r + 16, place, lane_tile(c)] = jnp.swapaxes(block, 0, 1)
            return 0

        lax.fori_loop(0, units // 16, some_units, 0)
        stores[i].start()
    for store in stores:
        store.wait()


def by_row(weight, half, pieces=4):
    units, rows, cols = weight.shape
    units = units // 2
    return pl.pallas_call(
        functools.partial(by_row_kernel, half * units),
        in_specs=[far],
        out_specs=far,
        out_shape=jax.ShapeDtypeStruct((rows, units, cols), BF16),
        scratch_shapes=[
            pltpu.VMEM((pieces, units // pieces, rows, cols), BF16),
            pltpu.VMEM((pieces, rows, units // pieces, cols), BF16),
            pltpu.SemaphoreType.DMA((pieces,)),
            pltpu.SemaphoreType.DMA((pieces,)),
        ],
        compiler_params=params(),
        cost_estimate=pl.CostEstimate(
            flops=0, bytes_accessed=4 * units * rows * cols, transcendentals=0
        ),
    )(weight)


def forward(seed_ref, first_ref, second_ref, third_ref, inputs, act_a, act_b, hidden, gate, raw):
    devices = seed_ref.shape[0]
    here = inputs.shape[0] // devices
    for d in range(devices):
        raw[d * here : (d + 1) * here, :] = seed_ref[d, :here, :]
    inputs[...] = raw[...].astype(BF16)
    act = jnp.tanh(dot(inputs[...], first_ref[...]))
    act_a[...] = act
    act = jnp.tanh(dot(act.astype(BF16), second_ref[...]))
    act_b[...] = act
    act = jnp.tanh(dot(act.astype(BF16), third_ref[...]))
    hidden[...] = act.astype(BF16)
    gate[...] = 1.0 - act * act


def main_kernel(
    scale, snaps, own_far, top_far, bottom_far, seed_far, low_far, high_far, assign_far, first_far, second_far, third_far,
    res_far, back_ref, in_far, a_far, b_far, hid_far,
    state, rate, history, picked, predicted, by_rows, total, raw, assigned, first, second, third,
    own_ref, top_ref, bottom_ref, seed_ref, gather, gate, res, inputs, act_a, act_b, hidden, arrived, filled, left,
):
    fields, _, rows, width = own_ref.shape
    _, batch, cols = predicted.shape
    units = by_rows.shape[1]
    tiles = width // LANES
    entries = fields * STEPS
    pitch = entries + 1
    pairs = (
        (top_far, top_ref), (own_far, own_ref), (bottom_far, bottom_ref),
        (seed_far, seed_ref), (first_far, first), (second_far, second), (third_far, third), (assign_far, assigned),
    )
    loads = [
        pltpu.make_async_copy(source, target, arrived.at[i])
        for i, (source, target) in enumerate(pairs)
    ]
    for load in loads:
        load.start()
    together = 2 if fields % 2 == 0 else 1
    parts = STEPS // 8
    turns = fields // together * parts
    fills = [
        [
            pltpu.make_async_copy(
                source.at[low : low + 4],
                by_rows.at[low : low + 4, half * units // 2 : (half + 1) * units // 2, :],
                filled.at[half, low // 4],
            )
            for half, source in enumerate((low_far, high_far))
        ]
        for low in range(0, rows, 4)
    ]
    place = lax.broadcasted_iota(jnp.int32, (width, cols), 0)
    column = lax.broadcasted_iota(jnp.int32, (width, cols), 1) + STEPS
    gather[...] = (tiles * (place % LANES) + place // LANES == column).astype(F32).astype(BF16)
    for load in loads[:3]:
        load.wait()
    for pair in fills:
        for fill in pair:
            fill.start()

    for f in range(fields):
        for now in range(2):
            for j in range(tiles):
                state[f, now, j, :8, :] = jnp.zeros((8, LANES), F32)
                state[f, now, j, 8 + 3 * rows :, :] = jnp.zeros((8, LANES), F32)
        for j in range(tiles):
            for place, ref in enumerate((top_ref, own_ref, bottom_ref)):
                low = 8 + place * rows
                state[f, 0, j, low : low + rows, :] = ref[f, 0, :, lane_tile(j)]
                rate[f, j, low : low + rows, :] = ref[f, 1, :, lane_tile(j)]
                if place != 1:
                    state[f, 1, j, low : low + rows, :] = ref[f, 0, :, lane_tile(j)]
    def solve(turn, first_row):
        which = [turn // parts * together + i for i in range(together)]
        part = turn % parts

        def two_steps(pair, _):
            for now in range(2):
                advance(state, rate, history, pitch, part, which, now, 2 * pair + now)
            if first_row is not None:
                r = first_row + pair - 4 * part
                predicted[r] = dot(hidden[...], by_rows[r])
            return 0

        lax.fori_loop(4 * part, 4 * part + 4, two_steps, 0)

    which = list(range(together))
    for t in range(4):
        advance(state, rate, history, pitch, 0, which, t % 2, t)
    for load in loads[3:]:
        load.wait()
    forward(seed_ref, first, second, third, inputs, act_a, act_b, hidden, gate, raw)
    for t in range(4, 8):
        advance(state, rate, history, pitch, 0, which, t % 2, t)
    stores = [
        pltpu.make_async_copy(source, target, left.at[i])
        for i, (source, target) in enumerate(
            ((inputs, in_far), (act_a, a_far), (act_b, b_far), (hidden, hid_far))
        )
    ]
    for store in stores:
        store.start()
    for turn in range(1, turns):
        if turn <= len(fills):
            for fill in fills[turn - 1]:
                fill.wait()
        solve(turn, 4 * (turn - 1) if turn <= len(fills) else None)
    for turn in range(turns, len(fills) + 1):
        for fill in fills[turn - 1]:
            fill.wait()
        for r in range(4 * (turn - 1), 4 * turn):
            predicted[r] = dot(hidden[...], by_rows[r])

    lane = lax.broadcasted_iota(jnp.int32, (snaps, entries), 1)
    steps = []
    for f in range(fields):
        last = own_ref[f, 0, :snaps, META : META + 1].astype(jnp.int32)
        steps.append((lane == f * STEPS + last).astype(F32))
    steps = jnp.concatenate(steps, axis=0).astype(BF16)
    number = lax.broadcasted_iota(jnp.int32, (fields * snaps, batch), 0)
    chosen = (number == assigned[...]).astype(F32).astype(BF16)
    hot = contract_rows(chosen, steps).astype(BF16)
    chunk = 8
    for i in range(rows // chunk):
        for k in range(chunk):
            low = (i * chunk + k) * pitch
            for j in range(tiles):
                states = history[j, low : low + entries, :].astype(BF16)
                picked[i % 2, k * batch : (k + 1) * batch, lane_tile(j)] = dot(hot, states).astype(BF16)
        targets = dot(picked[i % 2], gather[...])
        for k in range(chunk):
            r = i * chunk + k
            residual = ((predicted[r] - targets[k * batch : (k + 1) * batch]) * scale).astype(BF16)
            res[r] = residual
            part = contract_cols(residual, by_rows[r])
            back = part if k == 0 else back + part
        total[...] = back if i == 0 else total[...] + back
        place = slice(i * chunk, (i + 1) * chunk)
        stores.append(pltpu.make_async_copy(res.at[place], res_far.at[place], left.at[4 + i]))
        stores[-1].start()
    total[...] = total[...] * gate[...]
    fold_rows(total, back_ref)
    for store in stores:
        store.wait()


def main(assign, own, top, bottom, seeds, w_first, w_second, w_third, halves, snaps, here, fold):
    rows, units, cols = halves[0].shape
    units = 2 * units
    features = w_first.shape[0]
    devices = seeds.shape[0]
    batch = devices * here
    fields, _, _, width = own.shape
    tiles = width // LANES
    depth = 3 * rows + 16
    entries = fields * STEPS
    scale = 1.0 / float(batch) ** 0.5
    folded = (devices, here * fold, units // fold)
    kept = [
        ((rows, batch, cols), BF16),
        ((batch, features), BF16),
        ((batch, units), F32),
        ((batch, units), F32),
        ((batch, units), BF16),
    ]
    shapes = [jax.ShapeDtypeStruct(*k) for k in kept]
    return pl.pallas_call(
        functools.partial(main_kernel, scale, snaps),
        in_specs=[far] * 10,
        out_specs=[far, whole] + [far] * 4,
        out_shape=[shapes[0], jax.ShapeDtypeStruct(folded, F32)] + shapes[1:],
        scratch_shapes=[
            pltpu.VMEM((fields, 2, tiles, depth, LANES), F32),
            pltpu.VMEM((fields, tiles, depth, LANES), F32),
            pltpu.VMEM((tiles, (rows + 1) * (entries + 1), LANES), F32),
            pltpu.VMEM((2, 8 * batch, width), BF16),
            pltpu.VMEM((rows, batch, cols), F32),
            pltpu.VMEM((rows, units, cols), BF16),
            pltpu.VMEM((batch, units), F32),
            pltpu.VMEM((batch, features), F32),
            pltpu.VMEM((1, batch), jnp.int32),
            pltpu.VMEM(w_first.shape, BF16),
            pltpu.VMEM(w_second.shape, BF16),
            pltpu.VMEM(w_third.shape, BF16),
            pltpu.VMEM(own.shape, F32),
            pltpu.VMEM(own.shape, F32),
            pltpu.VMEM(own.shape, F32),
            pltpu.VMEM(seeds.shape, F32),
            pltpu.VMEM((width, cols), BF16),
            pltpu.VMEM((batch, units), F32),
        ]
        + [pltpu.VMEM(*k) for k in kept]
        + [
            pltpu.SemaphoreType.DMA((8,)),
            pltpu.SemaphoreType.DMA((2, rows // 4)),
            pltpu.SemaphoreType.DMA((4 + rows // 8,)),
        ],
        compiler_params=params(),
    )(own, top, bottom, seeds, *halves, assign.reshape(1, batch), w_first, w_second, w_third)


def outer_kernel(hid_ref, res_ref, out_ref, grads):
    rows, _, cols = res_ref.shape
    units = out_ref.shape[0]
    for r in range(rows):
        grads[r] = contract_rows(hid_ref[...], res_ref[r]).astype(BF16)
    for c in range(cols // LANES):
        for u in range(0, units, 16):
            for r in range(0, rows, 16):
                block = grads[r : r + 16, u : u + 16, lane_tile(c)]
                out_ref[u : u + 16, r : r + 16, lane_tile(c)] = jnp.swapaxes(block, 0, 1)


def outer(hidden, res, chunk=128):
    rows, batch, cols = res.shape
    units = hidden.shape[1]
    return pl.pallas_call(
        outer_kernel,
        grid=(units // chunk,),
        in_specs=[
            pl.BlockSpec((batch, chunk), lambda i: (0, i)),
            pl.BlockSpec((rows, batch, cols), lambda i: (0, 0, 0)),
        ],
        out_specs=pl.BlockSpec((chunk, rows, cols), lambda i: (i, 0, 0)),
        out_shape=jax.ShapeDtypeStruct((units, rows, cols), BF16),
        scratch_shapes=[pltpu.VMEM((rows, chunk, cols), BF16)],
        compiler_params=params(),
        cost_estimate=pl.CostEstimate(
            flops=2 * batch * units * rows * cols,
            bytes_accessed=4 * units * rows * cols,
            transcendentals=0,
        ),
    )(hidden, res)


def delta_kernel(pieces, out_ref):
    devices = pieces.shape[0]
    delta = [pieces[d] for d in range(devices)]
    while len(delta) > 1:
        delta = [a + b for a, b in zip(delta[::2], delta[1::2])] + delta[len(delta) // 2 * 2 :]
    delta = delta[0].astype(BF16)
    for d in range(devices):
        out_ref[d] = delta


def delta_spread(pieces):
    return pl.pallas_call(
        delta_kernel,
        in_specs=[whole],
        out_specs=whole,
        out_shape=jax.ShapeDtypeStruct(pieces.shape, BF16),
        compiler_params=params(16384),
    )(pieces)


def backward_kernel(
    inputs_far, a_far, b_far, delta_far, second_far, third_far, g1_far, g2_far, g3_far,
    inputs, act_a, act_b, folded, second, third, wide, unfolded, g1, g2, g3, arrived, left,
):
    pairs = (
        (delta_far, folded), (b_far, act_b), (third_far, third),
        (a_far, act_a), (second_far, second), (inputs_far, inputs),
    )
    loads = [
        pltpu.make_async_copy(source, target, arrived.at[i])
        for i, (source, target) in enumerate(pairs)
    ]
    for load in loads:
        load.start()
    stores = [
        pltpu.make_async_copy(source, target, left.at[i])
        for i, (source, target) in enumerate(((g3, g3_far), (g2, g2_far), (g1, g1_far)))
    ]
    devices, deep, width = folded.shape
    batch, units = act_a.shape
    here = batch // devices
    loads[0].wait()
    wide[...] = folded[...].astype(F32)
    for d in range(devices):
        for k in range(units // width):
            unfolded[d * here : (d + 1) * here, k * width : (k + 1) * width] = wide[
                d, k * here : (k + 1) * here, :
            ]
    delta = unfolded[...].astype(BF16)
    loads[1].wait()
    act = act_b[...]
    g3[...] = contract_rows(act.astype(BF16), delta)
    stores[0].start()
    loads[2].wait()
    delta = (contract_cols(delta, third[...]) * (1.0 - act * act)).astype(BF16)
    loads[3].wait()
    act = act_a[...]
    g2[...] = contract_rows(act.astype(BF16), delta)
    stores[1].start()
    loads[4].wait()
    delta = (contract_cols(delta, second[...]) * (1.0 - act * act)).astype(BF16)
    loads[5].wait()
    g1[...] = contract_rows(inputs[...], delta)
    stores[2].start()
    for store in stores:
        store.wait()


def backward(inputs, act_a, act_b, delta, w_second, w_third):
    batch, units = act_a.shape
    shapes = [(inputs.shape[1], units), (units, units), (units, units)]
    return pl.pallas_call(
        backward_kernel,
        in_specs=[far] * 6,
        out_specs=[far] * 3,
        out_shape=[jax.ShapeDtypeStruct(shape, F32) for shape in shapes],
        scratch_shapes=[
            pltpu.VMEM(inputs.shape, BF16),
            pltpu.VMEM(act_a.shape, F32),
            pltpu.VMEM(act_b.shape, F32),
            pltpu.VMEM(delta.shape, BF16),
            pltpu.VMEM(w_second.shape, BF16),
            pltpu.VMEM(w_third.shape, BF16),
            pltpu.VMEM(delta.shape, F32),
            pltpu.VMEM((batch, units), F32),
        ]
        + [pltpu.VMEM(shape, F32) for shape in shapes]
        + [pltpu.SemaphoreType.DMA((6,)), pltpu.SemaphoreType.DMA((3,))],
        compiler_params=params(),
    )(inputs, act_a, act_b, delta, w_second, w_third)


def swap(value, axes):
    return lax.all_to_all(value, axes, split_axis=0, concat_axis=0, tiled=True)


def per_device(
    initial,
    conductivity,
    step_count,
    emit_steps,
    assign,
    sample_inputs,
    w_first,
    w_second,
    w_third,
    w_out,
):
    groups, strips = lax.axis_size("group"), lax.axis_size("strip")
    devices = groups * strips
    here = sample_inputs.shape[0]
    fold = max(1, 16 // here)
    blocks, seeds = split_columns(
        initial, conductivity, step_count, emit_steps, sample_inputs, groups, devices
    )
    blocks, w_out = lax.optimization_barrier((blocks, w_out))
    own = swap(blocks, "group")
    low = by_row(w_out, 0)
    own, low, w_out = lax.optimization_barrier((own, low, w_out))
    down = [(i, i + 1) for i in range(strips - 1)]
    top = lax.ppermute(own, "strip", down)
    bottom = lax.ppermute(own, "strip", [(j, i) for i, j in down])
    own, seeds = lax.optimization_barrier((own, seeds))
    seeds = swap(seeds, ALL)
    res, partial, inputs, act_a, act_b, hidden = main(
        assign, own, top, bottom, seeds, w_first, w_second, w_third, (low, by_row(w_out, 1)),
        emit_steps.shape[1], here, fold,
    )
    pieces = swap(partial, ALL)
    grad_out = outer(hidden, res)
    pieces, grad_out = lax.optimization_barrier((pieces, grad_out))
    delta = swap(delta_spread(pieces), ALL)
    grads = backward(inputs, act_a, act_b, delta, w_second, w_third)
    return (*grads, grad_out)


def solution(mesh):
    placed = (
        P("group", "strip", None),
        P("group", "strip", None),
        P("group"),
        P("group", None),
        P(),
        P(("group", "strip"), None),
        P(),
        P(),
        P(),
        P(None, "strip", "group"),
    )
    return jax.shard_map(
        per_device,
        mesh=mesh,
        in_specs=placed,
        out_specs=(P(), P(), P(), P(None, "strip", "group")),
        check_vma=False,
    )
```
